128 devices in a mesh: dp: 8 (over y, core), expert: 16 (over z, x).
Axes of the slice: x: 4, y: 4, z: 4, core: 2. Of those that a mesh axis runs over, the one named last changes fastest.
Arguments:
- tokens: bfloat16 [16384, 2048], P(('dp', 'expert')), may hold values from -6 to 6
- expert_ids: int32 [16384], P(('dp', 'expert')), may hold values from 0 to 31, as said below
- gate_weights: float32 [16384], P(('dp', 'expert')), may hold values from 0.25 to 1
- in_weights: bfloat16 [32, 2048, 4096], P('expert', None, 'dp'), may hold values from -0.125 to 0.125
- out_weights: bfloat16 [32, 4096, 2048], P('expert', 'dp'), may hold values from -0.09375 to 0.09375
- cotangent: bfloat16 [16384, 2048], P(('dp', 'expert')), may hold values from -6 to 6
Outputs:
- mixed: bfloat16 [16384, 2048], P(('dp', 'expert'))
- gate_grad: float32 [16384], P(('dp', 'expert'))
- token_grad: bfloat16 [16384, 2048], P(('dp', 'expert'))
- in_weights_grad: bfloat16 [32, 2048, 4096], P('expert', None, 'dp')
- out_weights_grad: bfloat16 [32, 4096, 2048], P('expert', 'dp')
The draws below stay inside these ranges and needn't reach their ends.
Inputs may be any that keep to these rules, and one draw needn't show every extreme that they name: `expert_ids`: within each device's aligned block of 128 rows no expert is named more than 8 times, and one and the same expert is named exactly 8 times in every block; every expert is named somewhere.
All inputs are finite; a program needn't handle non-finite values.
Results may differ from the reference program's by a relative error of at most 0.015.
Values may be sent and summed in bfloat16 or wider, within the bound.
A program may use at most 192 MiB of HBM per device.

```python
import math
import jax
import jax.numpy as jnp
from jax import lax

D = 2048
FF = 4096
TOK_DEV = 128
EXPERTS = 32
TOKENS = 16384
CAP = 8
GROUPS = 8
N_DP = 8
N_EXPERT = 16


def draw_expert_ids(key, part):
    key = jax.random.fold_in(key, 17)
    key_favored, key_levels, key_scores, key_shuffle = jax.random.split(key, 4)
    blocks = N_DP * N_EXPERT
    pool_size = EXPERTS * CAP
    pool_index = jnp.arange(pool_size, dtype=jnp.int32)
    shared_pool_expert = pool_index // CAP
    leading_slot = pool_index % CAP == 0
    preferred_expert = jax.random.randint(key_favored, (), 0, EXPERTS, dtype=jnp.int32)
    priority_tiers = jax.random.randint(key_levels, (EXPERTS,), 0, 4, dtype=jnp.int32)
    jitter_amount = jax.random.randint(key_scores, (blocks, pool_size), 0, 1024, dtype=jnp.int32)
    extra_logit = jnp.where(shared_pool_expert == preferred_expert, 32768, jnp.where(leading_slot, 16384, 0)).astype(jnp.int32)
    router_logits = jitter_amount + priority_tiers[shared_pool_expert] * 1024 + extra_logit
    router_logits = router_logits * pool_size + pool_index
    chosen_vals, chosen = lax.top_k(router_logits, TOK_DEV)
    picked = shared_pool_expert[chosen]
    picked = jax.random.permutation(key_shuffle, picked, axis=1, independent=True)
    return picked.reshape(-1).astype(jnp.int32)


def levels(stream_key, extent, cuts, low, top_value):
    def one(position, parts):
        heights = jax.random.uniform(jax.random.fold_in(jax.random.fold_in(stream_key, 6), position), (parts,), jnp.float32, low / len(cuts), top_value / len(cuts))
        return jnp.repeat(jnp.exp(heights), extent[position] // parts).reshape((-1,) + (1,) * (len(extent) - position - 1))

    level = one(*cuts[0])
    for cut in cuts[1:]:
        level = level * one(*cut)
    return level


def noise(stream_key, dims, deviation, limit, cuts=(), held_as=jnp.bfloat16):
    level = levels(stream_key, dims, cuts, -0.22, 0.18) if cuts else 1.0
    drawn = jax.random.normal(stream_key, dims, jnp.float32) * deviation * level
    return jnp.minimum(jnp.maximum(drawn, -limit), limit).astype(held_as)


def setup_inputs(seed: int = 0) -> dict:
    key_of = jax.random.split(jax.random.key(seed), 7)
    tokens = noise(key_of[0], (TOKENS, D), 1.0, 6.0, ((0, 128),))
    expert_ids = draw_expert_ids(jax.random.fold_in(key_of[6], 71), 0)
    gate_weights = jnp.clip(jnp.exp(math.log(1.0) - 1.3862944 * jax.random.uniform(key_of[2], (TOKENS,), jnp.float32) ** levels(key_of[2], (TOKENS,), ((0, 128),), -0.2, 0.2)), 0.25, 1.0)
    in_weights = noise(key_of[3], (EXPERTS, D, FF), D ** -0.5, 0.125, ((0, 16), (2, 8)))
    out_weights = noise(key_of[4], (EXPERTS, FF, D), FF ** -0.5, 0.09375, ((0, 16), (1, 8)))
    cotangent = noise(key_of[5], (TOKENS, D), 1.0, 6.0, ((0, 128),))
    return {"tokens": tokens, "expert_ids": expert_ids, "gate_weights": gate_weights, "in_weights": in_weights, "out_weights": out_weights, "cotangent": cotangent}


root_half = 0.7071067811865476
inv_root_tau = 0.3989422804014327


def gelu_value(values):
    return 0.5 * values * (1.0 + lax.erf(values * root_half))


def gelu_slope(values):
    return 0.5 * (1.0 + lax.erf(values * root_half)) + values * jnp.exp(-0.5 * values * values) * inv_root_tau


def reference(tokens, expert_ids, gate_weights, in_weights, out_weights, cotangent):
    features = tokens.shape[1]
    group_width = FF // GROUPS
    slot_limit = CAP * N_DP * N_EXPERT
    sort_order = jnp.argsort(expert_ids, stable=True).astype(jnp.int32)
    onehot = (expert_ids[:, None] == jnp.arange(EXPERTS, dtype=jnp.int32)[None, :]).astype(jnp.int32)
    counts = jnp.sum(onehot, 0).astype(jnp.int32)
    offsets = (jnp.cumsum(counts) - counts).astype(jnp.int32)
    out_grad = (gate_weights[:, None] * cotangent.astype(jnp.float32)).astype(jnp.bfloat16)
    padding = jnp.zeros((slot_limit, features), jnp.bfloat16)
    sorted_x = jnp.concatenate([tokens[sort_order], padding], 0)
    sorted_g = jnp.concatenate([out_grad[sort_order], padding], 0)

    def per_expert(expert):
        first_row = offsets[expert]
        live_rows = (jnp.arange(slot_limit, dtype=jnp.int32) < counts[expert])[:, None]
        zero_value = jnp.zeros((), jnp.bfloat16)
        expert_x = jnp.where(live_rows, lax.dynamic_slice_in_dim(sorted_x, first_row, slot_limit, 0), zero_value)
        expert_g = jnp.where(live_rows, lax.dynamic_slice_in_dim(sorted_g, first_row, slot_limit, 0), zero_value)
        weight_in = in_weights[expert]
        weight_out = out_weights[expert]
        pre_act = jnp.dot(expert_x, weight_in, preferred_element_type=jnp.float32)
        hidden = gelu_value(pre_act).astype(jnp.bfloat16)

        def add_forward(group, running):
            columns = lax.dynamic_slice_in_dim(hidden, group * group_width, group_width, 1)
            weight_rows = lax.dynamic_slice_in_dim(weight_out, group * group_width, group_width, 0)
            partial_value = jnp.dot(columns, weight_rows, preferred_element_type=jnp.float32).astype(jnp.bfloat16)
            partial_value = lax.optimization_barrier(partial_value)
            return running + partial_value.astype(jnp.float32)

        expert_out = lax.fori_loop(0, GROUPS, add_forward, jnp.zeros((slot_limit, features), jnp.float32)).astype(jnp.bfloat16)
        hidden_back = jnp.dot(expert_g, weight_out.T, preferred_element_type=jnp.float32)
        hidden_grad = (hidden_back * gelu_slope(pre_act)).astype(jnp.bfloat16)
        out_grad_w = jnp.dot(hidden.T, expert_g, preferred_element_type=jnp.float32).astype(jnp.bfloat16)
        in_grad_w = jnp.dot(expert_x.T, hidden_grad, preferred_element_type=jnp.float32).astype(jnp.bfloat16)

        def add_backward(group, running):
            columns = lax.dynamic_slice_in_dim(hidden_grad, group * group_width, group_width, 1)
            weight_cols = lax.dynamic_slice_in_dim(weight_in, group * group_width, group_width, 1)
            partial_value = jnp.dot(columns, weight_cols.T, preferred_element_type=jnp.float32).astype(jnp.bfloat16)
            partial_value = lax.optimization_barrier(partial_value)
            return running + partial_value.astype(jnp.float32)

        token_back = lax.fori_loop(0, GROUPS, add_backward, jnp.zeros((slot_limit, features), jnp.float32)).astype(jnp.bfloat16)
        return expert_out, token_back, in_grad_w, out_grad_w

    stacked_out, stacked_back, in_weights_grad, out_weights_grad = lax.map(per_expert, jnp.arange(EXPERTS, dtype=jnp.int32))
    sorted_expert = expert_ids[sort_order]
    local_slot = jnp.arange(expert_ids.shape[0], dtype=jnp.int32) - offsets[sorted_expert]
    flat_index = (sorted_expert * slot_limit + local_slot).astype(jnp.int32)
    out_sorted = stacked_out.reshape(EXPERTS * slot_limit, features)[flat_index]
    back_sorted = stacked_back.reshape(EXPERTS * slot_limit, features)[flat_index]
    expert_out = jnp.zeros_like(tokens).at[sort_order].set(out_sorted)
    token_grad = jnp.zeros_like(tokens).at[sort_order].set(back_sorted)
    out_value = expert_out.astype(jnp.float32)
    mixed = (gate_weights[:, None] * out_value).astype(jnp.bfloat16)
    gate_grad = jnp.sum(cotangent.astype(jnp.float32) * out_value, 1)
    return mixed, gate_grad, token_grad, in_weights_grad, out_weights_grad
```

```python
import jax
import jax.numpy as jnp
from jax import lax
from jax.sharding import PartitionSpec as P

root_half = 0.7071067811865476
inv_root_tau = 0.3989422804014327


def gelu_value(values):
    return 0.5 * values * (1.0 + lax.erf(values * root_half))


def gelu_slope(values):
    return (
        0.5 * (1.0 + lax.erf(values * root_half))
        + values * jnp.exp(-0.5 * values * values) * inv_root_tau
    )


def route(rows, local_experts):
    ex_count = lax.axis_size("expert")
    experts, capacity, features = rows.shape
    by_expert = rows.reshape(ex_count, local_experts, capacity, features)
    gathered = []
    for f in range(local_experts):
        swapped = lax.all_to_all(by_expert[:, f], "expert", split_axis=0, concat_axis=0, tiled=True)
        gathered.append(
            lax.all_gather(swapped.reshape(ex_count * capacity, features), "dp", axis=0, tiled=True)
        )
    return gathered


def route_back(term, capacity):
    ex_count = lax.axis_size("expert")
    summed = lax.psum_scatter(term.astype(jnp.bfloat16), "dp", scatter_dimension=0, tiled=True)
    return lax.all_to_all(
        summed.reshape(ex_count, capacity, term.shape[1]), "expert", split_axis=0, concat_axis=0, tiled=True
    )


def local(tokens, expert_ids, gate_weights, in_weights, out_weights, cotangent):
    ex_count = lax.axis_size("expert")
    local_experts = in_weights.shape[0]
    experts = local_experts * ex_count
    token_count = tokens.shape[0]
    features = tokens.shape[1]
    capacity = 2 * token_count // experts
    onehot = (expert_ids[:, None] == jnp.arange(experts, dtype=jnp.int32)[None, :]).astype(
        jnp.int32
    )
    rank_before = jnp.cumsum(onehot, 0) - onehot
    slot_index = jnp.sum(rank_before * onehot, 1)
    target = expert_ids * capacity + slot_index
    placer = (jnp.arange(experts * capacity, dtype=jnp.int32)[:, None] == target[None, :]).astype(
        jnp.bfloat16
    )
    out_grad = (gate_weights[:, None] * cotangent.astype(jnp.float32)).astype(jnp.bfloat16)

    def place(rows):
        return (
            jnp.dot(placer, rows, preferred_element_type=jnp.float32)
            .astype(jnp.bfloat16)
            .reshape(experts, capacity, features)
        )

    routed_x = route(place(tokens), local_experts)
    routed_g = route(place(out_grad), local_experts)
    dot = lambda a, b, dims: lax.dot_general(a, b, (dims, ((), ())), preferred_element_type=jnp.float32)
    fwd, bwd, in_grads, out_grads = [], [], [], []
    for f in range(local_experts):
        pre_act = dot(routed_x[f], in_weights[f], ((1,), (0,)))
        hidden = gelu_value(pre_act).astype(jnp.bfloat16)
        fwd.append(route_back(dot(hidden, out_weights[f], ((1,), (0,))), capacity))
        hidden_back = dot(routed_g[f], out_weights[f], ((1,), (1,)))
        hidden_grad = (hidden_back * gelu_slope(pre_act)).astype(jnp.bfloat16)
        bwd.append(route_back(dot(hidden_grad, in_weights[f], ((1,), (1,))), capacity))
        out_grads.append(dot(hidden, routed_g[f], ((0,), (0,))).astype(jnp.bfloat16))
        in_grads.append(dot(routed_x[f], hidden_grad, ((0,), (0,))).astype(jnp.bfloat16))

    def unplace(parts):
        rows = jnp.stack(parts, 1).reshape(experts * capacity, features)
        return jnp.einsum("st,sd->td", placer, rows, preferred_element_type=jnp.float32)

    token_out = unplace(fwd)
    mixed = (gate_weights[:, None] * token_out).astype(jnp.bfloat16)
    gate_grad = jnp.sum(cotangent.astype(jnp.float32) * token_out, 1)
    token_grad = unplace(bwd).astype(jnp.bfloat16)
    return (mixed, gate_grad, token_grad, jnp.stack(in_grads), jnp.stack(out_grads))


def solution(mesh):
    in_specs = (
        P(("dp", "expert"), None),
        P(("dp", "expert")),
        P(("dp", "expert")),
        P("expert", None, "dp"),
        P("expert", "dp", None),
        P(("dp", "expert"), None),
    )
    out_specs = (
        P(("dp", "expert"), None),
        P(("dp", "expert")),
        P(("dp", "expert"), None),
        P("expert", None, "dp"),
        P("expert", "dp", None),
    )
    return jax.shard_map(local, mesh=mesh, in_specs=in_specs, out_specs=out_specs, check_vma=False)
```

```python
import functools

import jax
import jax.numpy as jnp
from jax import lax
from jax.experimental import pallas as pl
from jax.experimental.pallas import tpu as pltpu
from jax.sharding import PartitionSpec as P

root_half = 0.7071067811865476
inv_root_tau = 0.3989422804014327
MESH = pl.DeviceIdType.MESH
CAP = 8
UNIT = 2 * CAP
NY = 4
BF16, F32 = jnp.bfloat16, jnp.float32


def layer_kernel(
    plane,
    tok, cot, gate, ids, win_h, wout_h,
    mixed, ggrad, tgrad, dwin_h, dwout_h,
    X, G, win, wout, S, H, Pf, sib, rs, stage, aback, gown, sibx, sibg, sibids,
    swap_s, swap_r, w_s, a2a_s, a2a_r, ag_s, ag_r, sb_s, sb_r, ps_s, ps_r, rs_s, rs_r,
    bk_s, bk_r, fn_s, fn_r, out_s, credit,
):
    tokens, features = tok.shape
    block = UNIT * plane
    rows_all = NY * block
    hidden_width = win.shape[2]
    half_cols = features // 2
    tile_rows = rows_all // 2
    quarter = features // 4

    dp = lax.axis_index("dp")
    e = lax.axis_index("expert")
    y = dp // 2
    c = dp % 2
    o = 1 - c
    y_up, y_dn, y_far = (y + 1) % NY, (y + 3) % NY, (y + 2) % NY
    up, dn, twin = y_up * 2 + c, y_dn * 2 + c, y * 2 + o

    def remote(src, dst, ssem, rsem, to_dp, to_e=None):
        return pltpu.make_async_remote_copy(
            src_ref=src, dst_ref=dst, send_sem=ssem, recv_sem=rsem,
            device_id=(to_dp, e if to_e is None else to_e), device_id_type=MESH,
        )

    def wait_in(ref, sem):
        remote(ref, ref, sem, sem, dp).wait_recv()

    def wait_out(ref, sem):
        remote(ref, ref, sem, sem, dp).wait_send()

    def cols(h):
        return pl.ds(h * half_cols, half_cols)

    def block_rows(yb):
        return pl.ds(pl.multiple_of(yb * block, block), block)

    def unit_rows(start):
        return pl.ds(pl.multiple_of(start, UNIT), UNIT)

    load_in = pltpu.make_async_copy(win_h, win, w_s.at[0])
    load_out = pltpu.make_async_copy(wout_h, wout, w_s.at[1])
    load_in.start()
    load_out.start()

    barrier = pltpu.get_barrier_semaphore()

    def greet(k, carry):
        pl.semaphore_signal(barrier, inc=1, device_id=(dp, (e + k) % plane), device_id_type=MESH)
        return carry

    lax.fori_loop(1, plane, greet, 0)
    for other in (up, dn, twin):
        pl.semaphore_signal(barrier, inc=1, device_id=(other, e), device_id_type=MESH)

    gown[...] = (gate[...] * cot[...].astype(F32)).astype(BF16)

    def placer_of(id_rows, core):
        id_row = id_rows[0:1, :]
        n_experts = 2 * plane
        onehot = lax.broadcasted_iota(jnp.int32, (n_experts, tokens), 0) == id_row
        onehot_f = onehot.astype(F32)
        before = (
            lax.broadcasted_iota(jnp.int32, (tokens, tokens), 0)
            < lax.broadcasted_iota(jnp.int32, (tokens, tokens), 1)
        ).astype(F32).astype(BF16)
        rank = jnp.dot(onehot_f.astype(BF16), before, preferred_element_type=F32)
        slot = jnp.sum(rank * onehot_f, 0, keepdims=True).astype(jnp.int32)
        target = (id_row >> 1) * UNIT + core * CAP + slot
        target = jnp.where((id_row & 1) == c, target, -1)
        return (lax.broadcasted_iota(jnp.int32, (block, tokens), 0) == target).astype(F32).astype(BF16)

    placer_own = placer_of(ids[...], c)
    pl.semaphore_wait(barrier, plane + 2)

    swap = [
        remote(ids, sibids, swap_s.at[0], swap_r.at[0], twin),
        remote(tok, sibx, swap_s.at[1], swap_r.at[1], twin),
        remote(gown, sibg, swap_s.at[2], swap_r.at[2], twin),
    ]
    for copy in swap:
        copy.start()
    swap[0].wait_recv()
    placer_sib = placer_of(sibids[...], o)

    bufs = (X, G)
    own_src = (tok, gown)
    sib_src = (sibx, sibg)

    def place_and_send(a, h):
        placed = jnp.dot(placer_own, own_src[a][:, cols(h)], preferred_element_type=F32)
        placed += jnp.dot(placer_sib, sib_src[a][:, cols(h)], preferred_element_type=F32)
        stage[a, :, cols(h)] = placed.astype(BF16)

        def landing(sender):
            return bufs[a].at[c, unit_rows(y * block + sender * UNIT), cols(h)]

        pltpu.make_async_copy(stage.at[a, unit_rows(e * UNIT), cols(h)], landing(e), a2a_r.at[a, h]).start()

        def send(k, carry):
            to = (e + k) % plane
            remote(
                stage.at[a, unit_rows(to * UNIT), cols(h)], landing(e),
                a2a_s.at[a, h], a2a_r.at[a, h], dp, to,
            ).start()
            return carry

        lax.fori_loop(1, plane, send, 0)

    swap[1].wait_recv()
    place_and_send(0, 0)
    place_and_send(0, 1)
    swap[2].wait_recv()
    place_and_send(1, 0)
    place_and_send(1, 1)

    twin_pieces = ((y, 0), (y, 1), (y_dn, 0), (y_up, 1), (y_dn, 1), (y_up, 0), (y_far, 0), (y_far, 1))
    ring_pieces = ((y_dn, 0), (y_dn, 1), (y_up, 0), (y_up, 1), (y_far, 0), (y_far, 1))
    ring_to_twin = (2, 4, 5, 3, 6, 7)

    def piece(a, f, where):
        return bufs[a].at[f, block_rows(where[0]), cols(where[1])]

    def to_twin(a, k):
        ref = piece(a, c, twin_pieces[k])
        remote(ref, ref, sb_s.at[a, k], sb_r.at[a, k], twin).start()

    def send_own(a, h):
        ref = piece(a, c, (y, h))
        wait_in(ref, a2a_r.at[a, h])
        remote(ref, ref, ag_s.at[a, h], ag_r.at[a, h], up).start()
        remote(ref, ref, ag_s.at[a, 2 + h], ag_r.at[a, 2 + h], dn).start()
        to_twin(a, h)

    def arrived(a, i):
        ref = piece(a, c, ring_pieces[i])
        wait_in(ref, ag_r.at[a, i])
        if i == 0:
            remote(ref, ref, ag_s.at[a, 4], ag_r.at[a, 4], up).start()
        if i == 3:
            remote(ref, ref, ag_s.at[a, 5], ag_r.at[a, 5], dn).start()
        to_twin(a, ring_to_twin[i])

    def wait_twin(a):
        for k in range(8):
            wait_in(piece(a, o, twin_pieces[k]), sb_r.at[a, k])

    def wait_gather_sends(a):
        for h in range(2):
            wait_out(piece(a, c, (y, h)), ag_s.at[a, h])
            wait_out(piece(a, c, (y, h)), ag_s.at[a, 2 + h])
            wait_out(piece(a, c, (y, h)), ag_s.at[a, 4 + h])
        for k in range(8):
            wait_out(piece(a, c, (y, 0)), sb_s.at[a, k])

    send_own(0, 0)
    send_own(0, 1)
    arrived(0, 0)
    arrived(0, 3)
    send_own(1, 0)
    send_own(1, 1)
    arrived(0, 1)
    arrived(0, 2)
    arrived(0, 4)
    arrived(0, 5)

    def tile(t):
        return pl.ds(pl.multiple_of(t * tile_rows, tile_rows), tile_rows)

    def forward(f):
        def step(t, carry):
            rows = tile(t)
            pre = jnp.dot(X[f, rows, :], win[f], preferred_element_type=F32)
            cdf = 0.5 * (1.0 + lax.erf(pre * root_half))
            hid = (pre * cdf).astype(BF16)
            H[f, rows, :] = hid
            S[f, rows, :] = (cdf + pre * jnp.exp(-0.5 * pre * pre) * inv_root_tau).astype(BF16)
            for n in range(4):
                at = pl.ds(n * quarter, quarter)
                Pf[f, rows, at] = jnp.dot(hid, wout[f, :, at], preferred_element_type=F32).astype(BF16)
            return carry

        lax.fori_loop(0, 2, step, 0)

    sums = (Pf, G)

    def partial_to_twin(d):
        for t in range(2):
            remote(sums[d].at[o, tile(t)], sib.at[tile(t)], ps_s.at[d, t], ps_r.at[d, t], twin).start()

    def wait_partial_sends(d):
        for t in range(2):
            wait_out(sib.at[tile(t)], ps_s.at[d, t])

    def total(d, where):
        return sums[d].at[c, block_rows(where[0]), cols(where[1])]

    def rs_send(d, i, where, to):
        remote(total(d, where), rs.at[d, i], rs_s.at[d, i], rs_r.at[d, i], to).start()

    def add_twin(d, yb):
        rows = block_rows(yb)
        for h in range(2):
            sums[d][c, rows, cols(h)] = (
                sums[d][c, rows, cols(h)].astype(F32) + sib[rows, cols(h)].astype(F32)
            ).astype(BF16)

    def add_ring(d, where, i):
        wait_in(rs.at[d, i], rs_r.at[d, i])
        rows, h = block_rows(where[0]), where[1]
        sums[d][c, rows, cols(h)] = (
            sums[d][c, rows, cols(h)].astype(F32) + rs[d, i].astype(F32)
        ).astype(BF16)

    def reduce_start(d):
        for t in range(2):
            wait_in(sib.at[tile(t)], ps_r.at[d, t])
        add_twin(d, y_far)
        rs_send(d, 0, (y_far, 0), up)
        rs_send(d, 3, (y_far, 1), dn)
        add_twin(d, y_up)
        rs_send(d, 1, (y_up, 1), up)
        add_twin(d, y_dn)
        rs_send(d, 4, (y_dn, 0), dn)
        add_twin(d, y)

    def reduce_middle(d):
        add_ring(d, (y_up, 0), 0)
        rs_send(d, 2, (y_up, 0), up)
        add_ring(d, (y_dn, 1), 3)
        rs_send(d, 5, (y_dn, 1), dn)

    def reduce_end(d, h):
        ins = ((4, 2), (1, 5))[h]
        rows = block_rows(y)
        for i in ins:
            wait_in(rs.at[d, i], rs_r.at[d, i])
        sums[d][c, rows, cols(h)] = (
            sums[d][c, rows, cols(h)].astype(F32) + rs[d, ins[0]].astype(F32) + rs[d, ins[1]].astype(F32)
        ).astype(BF16)

        def leaving(to):
            return sums[d].at[c, unit_rows(y * block + to * UNIT), cols(h)]

        landing = aback.at[d, unit_rows(e * UNIT), cols(h)]
        pltpu.make_async_copy(leaving(e), landing, bk_r.at[d, h]).start()

        def send(k, carry):
            to = (e + k) % plane
            remote(leaving(to), landing, bk_s.at[d, h], bk_r.at[d, h], dp, to).start()
            return carry

        lax.fori_loop(1, plane, send, 0)

    kept = (mixed, tgrad)
    other_sum = (sibx, sibg)

    def unplace(d, h):
        wait_in(aback.at[d, :, cols(h)], bk_r.at[d, h])
        routed = aback[d, :, cols(h)]
        dims = (((0,), (0,)), ((), ()))
        leave = stage.at[d, pl.ds(0, tokens), cols(h)]
        leave[...] = lax.dot_general(placer_sib, routed, dims, preferred_element_type=F32).astype(BF16)
        remote(leave, other_sum[d].at[:, cols(h)], fn_s.at[d, h], fn_r.at[d, h], twin).start()
        kept[d][:, cols(h)] = lax.dot_general(placer_own, routed, dims, preferred_element_type=F32).astype(BF16)

    def token_rows(d, h):
        wait_in(other_sum[d].at[:, cols(h)], fn_r.at[d, h])
        return kept[d][:, cols(h)].astype(F32) + other_sum[d][:, cols(h)].astype(F32)

    load_in.wait()
    load_out.wait()
    wait_twin(0)
    forward(o)
    partial_to_twin(0)
    arrived(1, 0)
    arrived(1, 3)
    forward(c)
    arrived(1, 1)
    arrived(1, 2)
    reduce_start(0)
    pl.semaphore_signal(credit, inc=1, device_id=(twin, e), device_id_type=MESH)
    arrived(1, 4)
    arrived(1, 5)

    transposed = (((1,), (1,)), ((), ()))
    over_rows = (((0,), (0,)), ((), ()))

    def hidden_back(f):
        def step(t, carry):
            rows = tile(t)
            back = lax.dot_general(G[f, rows, :], wout[f], transposed, preferred_element_type=F32)
            H[f, rows, :] = (back * S[f, rows, :].astype(F32)).astype(BF16)
            return carry

        lax.fori_loop(0, 2, step, 0)

    def token_back(f):
        def step(t, carry):
            rows = tile(t)
            for n in range(4):
                at = pl.ds(n * quarter, quarter)
                G[f, rows, at] = lax.dot_general(
                    H[f, rows, :], win[f, at, :], transposed, preferred_element_type=F32
                ).astype(BF16)
            return carry

        lax.fori_loop(0, 2, step, 0)

    def out_weights_tile(f, n):
        at = pl.ds(pl.multiple_of(n * quarter, quarter), quarter)
        Pf[o, pl.ds(pl.multiple_of(f * hidden_width, hidden_width), hidden_width), at] = lax.dot_general(
            H[f], G[f, :, at], over_rows, preferred_element_type=F32
        ).astype(BF16)

    def in_weights_spot(f, m):
        return (
            o,
            pl.ds(pl.multiple_of(f * quarter, quarter), quarter),
            pl.ds(pl.multiple_of(m * hidden_width, hidden_width), hidden_width),
        )

    def in_weights_tile(f, m):
        at = pl.ds(pl.multiple_of(m * quarter, quarter), quarter)
        Pf[in_weights_spot(f, m)] = lax.dot_general(
            X[f, :, at], H[f], over_rows, preferred_element_type=F32
        ).astype(BF16)

    wait_twin(1)
    wait_partial_sends(0)

    def out_tiles(f):
        def step(n, carry):
            out_weights_tile(f, n)
            return carry

        lax.fori_loop(0, 4, step, 0)

    out_tiles(o)
    reduce_middle(0)
    out_tiles(c)
    out_copies = [
        pltpu.make_async_copy(Pf.at[o, pl.ds(f * hidden_width, hidden_width)], dwout_h.at[f], out_s.at[f])
        for f in range(2)
    ]
    for copy in out_copies:
        copy.start()
    hidden_back(o)
    hidden_back(c)
    wait_gather_sends(1)
    token_back(o)
    pl.semaphore_wait(credit, 1)
    partial_to_twin(1)
    token_back(c)
    reduce_start(1)
    reduce_end(0, 0)
    reduce_end(0, 1)
    for copy in out_copies:
        copy.wait()

    def in_tiles(f):
        def step(m, carry):
            in_weights_tile(f, m)
            return carry

        lax.fori_loop(0, 4, step, 0)
        for m in range(4):
            pltpu.make_async_copy(
                Pf.at[in_weights_spot(f, m)], dwin_h.at[f, pl.ds(m * quarter, quarter)], out_s.at[2 + 4 * f + m]
            ).start()

    sent_rows = UNIT * (plane - 1)
    for a in range(2):
        for h in range(2):
            wait_out(stage.at[a, pl.ds(0, sent_rows), cols(h)], a2a_s.at[a, h])
    for copy in swap:
        copy.wait_send()
    wait_partial_sends(1)

    in_tiles(0)
    reduce_middle(1)
    unplace(0, 0)
    unplace(0, 1)
    in_tiles(1)
    gate_total = jnp.zeros((tokens, 1), F32)
    for h in range(2):
        out_rows = token_rows(0, h)
        gate_total += jnp.sum(cot[:, cols(h)].astype(F32) * out_rows, 1, keepdims=True)
        mixed[:, cols(h)] = (gate[...] * out_rows).astype(BF16)
    ggrad[...] = gate_total
    reduce_end(1, 0)
    reduce_end(1, 1)
    unplace(1, 0)
    unplace(1, 1)
    for h in range(2):
        tgrad[:, cols(h)] = token_rows(1, h).astype(BF16)

    wait_gather_sends(0)
    for f in range(2):
        for m in range(4):
            pltpu.make_async_copy(
                Pf.at[in_weights_spot(f, m)], dwin_h.at[f, pl.ds(m * quarter, quarter)], out_s.at[2 + 4 * f + m]
            ).wait()
    for d in range(2):
        for i in range(6):
            wait_out(rs.at[d, i], rs_s.at[d, i])
        for h in range(2):
            wait_out(aback.at[d, pl.ds(0, sent_rows), cols(h)], bk_s.at[d, h])
            wait_out(stage.at[d, pl.ds(0, tokens), cols(h)], fn_s.at[d, h])


def local(tokens, expert_ids, gate_weights, in_weights, out_weights, cotangent):
    plane = lax.axis_size("expert")
    count, features = tokens.shape
    hidden_width = in_weights.shape[2]
    block = UNIT * plane
    rows_all = NY * block
    half_cols = features // 2
    vmem = pl.BlockSpec(memory_space=pltpu.VMEM)
    hbm = pl.BlockSpec(memory_space=pl.ANY)
    dma = pltpu.SemaphoreType.DMA
    mixed, gate_grad, token_grad, in_grad, out_grad = pl.pallas_call(
        functools.partial(layer_kernel, plane),
        out_shape=(
            jax.ShapeDtypeStruct((count, features), BF16),
            jax.ShapeDtypeStruct((count, 1), F32),
            jax.ShapeDtypeStruct((count, features), BF16),
            jax.ShapeDtypeStruct(in_weights.shape, BF16),
            jax.ShapeDtypeStruct(out_weights.shape, BF16),
        ),
        in_specs=[vmem, vmem, vmem, vmem, hbm, hbm],
        out_specs=(vmem, vmem, vmem, hbm, hbm),
        scratch_shapes=[
            pltpu.VMEM((2, rows_all, features), BF16),
            pltpu.VMEM((2, rows_all, features), BF16),
            pltpu.VMEM(in_weights.shape, BF16),
            pltpu.VMEM(out_weights.shape, BF16),
            pltpu.VMEM((2, rows_all, hidden_width), BF16),
            pltpu.VMEM((2, rows_all, hidden_width), BF16),
                pltpu.VMEM((2, rows_all, features), BF16),
            pltpu.VMEM((rows_all, features), BF16),
            pltpu.VMEM((2, 6, block, half_cols), BF16),
            pltpu.VMEM((2, block, features), BF16),
            pltpu.VMEM((2, block, features), BF16),
            pltpu.VMEM((count, features), BF16),
            pltpu.VMEM((count, features), BF16),
            pltpu.VMEM((count, features), BF16),
            pltpu.VMEM((8, count), jnp.int32),
            dma((3,)), dma((3,)), dma((2,)),
            dma((2, 2)), dma((2, 2)),
            dma((2, 6)), dma((2, 6)),
            dma((2, 8)), dma((2, 8)),
            dma((2, 2)), dma((2, 2)),
            dma((2, 6)), dma((2, 6)),
            dma((2, 2)), dma((2, 2)),
            dma((2, 2)), dma((2, 2)),
            dma((10,)),
            pltpu.SemaphoreType.REGULAR,
        ],
        compiler_params=pltpu.CompilerParams(
            collective_id=0, has_side_effects=True, vmem_limit_bytes=60 * 1024 * 1024
        ),
    )(
        tokens, cotangent, gate_weights[:, None],
        jnp.broadcast_to(expert_ids[None], (8, count)), in_weights, out_weights,
    )
    return mixed, gate_grad[:, 0], token_grad, in_grad, out_grad


def solution(mesh):
    in_specs = (
        P(("dp", "expert"), None),
        P(("dp", "expert")),
        P(("dp", "expert")),
        P("expert", None, "dp"),
        P("expert", "dp", None),
        P(("dp", "expert"), None),
    )
    out_specs = (
        P(("dp", "expert"), None),
        P(("dp", "expert")),
        P(("dp", "expert"), None),
        P("expert", None, "dp"),
        P("expert", "dp", None),
    )
    return jax.shard_map(local, mesh=mesh, in_specs=in_specs, out_specs=out_specs, check_vma=False)
```

```python
import functools

import jax
import jax.numpy as jnp
from jax import lax
from jax.experimental import pallas as pl
from jax.experimental.pallas import tpu as pltpu
from jax.sharding import PartitionSpec as P

root_half = 0.7071067811865476
inv_root_tau = 0.3989422804014327
MESH = pl.DeviceIdType.MESH
CAP = 8
UNIT = 2 * CAP
NY = 4
CHUNKS = 4
BF16, F32 = jnp.bfloat16, jnp.float32


def layer_kernel(
    plane,
    tok, cot, gate, ids, win_h, wout_h,
    mixed, ggrad, tgrad, dwin_h, dwout_h,
    XG, win, wout, S, H, Pf, sib, rs, stage, aback, gown, sibx, sibg, sibids,
    swap_s, swap_r, w_s, a2a_s, a2a_r, ag_s, ag_r, sb_s, sb_r, ps_s, ps_r, rs_s, rs_r,
    bk_s, bk_r, fn_s, fn_r, out_s, credit,
):
    tokens, features = tok.shape
    block = UNIT * plane
    rows_all = NY * block
    hidden_width = win.shape[2]
    tile_rows = rows_all // 2
    quarter = features // CHUNKS
    eighth = quarter // 2
    X, G = XG.at[0], XG.at[1]

    dp = lax.axis_index("dp")
    e = lax.axis_index("expert")
    y = dp // 2
    c = dp % 2
    o = 1 - c
    y_up, y_dn, y_far = (y + 1) % NY, (y + 3) % NY, (y + 2) % NY
    up, dn, twin = y_up * 2 + c, y_dn * 2 + c, y * 2 + o

    def remote(src, dst, ssem, rsem, to_dp, to_e=None):
        return pltpu.make_async_remote_copy(
            src_ref=src, dst_ref=dst, send_sem=ssem, recv_sem=rsem,
            device_id=(to_dp, e if to_e is None else to_e), device_id_type=MESH,
        )

    def wait_in(ref, sem):
        remote(ref, ref, sem, sem, dp).wait_recv()

    def wait_out(ref, sem):
        remote(ref, ref, sem, sem, dp).wait_send()

    def cols(k):
        return pl.ds(k * quarter, quarter)

    def part(k, h):
        return pl.ds(k * quarter + h * eighth, eighth)

    def block_rows(yb):
        return pl.ds(pl.multiple_of(yb * block, block), block)

    def unit_rows(start):
        return pl.ds(pl.multiple_of(start, UNIT), UNIT)

    load_in = pltpu.make_async_copy(win_h, win, w_s.at[0])
    load_out = pltpu.make_async_copy(wout_h, wout, w_s.at[1])

    barrier = pltpu.get_barrier_semaphore()

    def greet(k, carry):
        pl.semaphore_signal(barrier, inc=1, device_id=(dp, (e + k) % plane), device_id_type=MESH)
        return carry

    for other in (twin, up, dn):
        pl.semaphore_signal(barrier, inc=1, device_id=(other, e), device_id_type=MESH)
    lax.fori_loop(1, plane, greet, 0)

    diagonal = lax.broadcasted_iota(jnp.int32, (tokens, tokens), 0) == lax.broadcasted_iota(
        jnp.int32, (tokens, tokens), 1
    )
    gate_col = jnp.sum(jnp.where(diagonal, gate[...], 0.0), 1, keepdims=True)
    gown[...] = (gate_col * cot[...].astype(F32)).astype(BF16)

    def placer_of(id_row, core):
        n_experts = 2 * plane
        onehot = lax.broadcasted_iota(jnp.int32, (n_experts, tokens), 0) == id_row
        onehot_f = onehot.astype(F32)
        before = (
            lax.broadcasted_iota(jnp.int32, (tokens, tokens), 0)
            < lax.broadcasted_iota(jnp.int32, (tokens, tokens), 1)
        ).astype(F32).astype(BF16)
        rank = jnp.dot(onehot_f.astype(BF16), before, preferred_element_type=F32)
        slot = jnp.sum(rank * onehot_f, 0, keepdims=True).astype(jnp.int32)
        target = (id_row >> 1) * UNIT + core * CAP + slot
        target = jnp.where((id_row & 1) == c, target, -1)
        return (lax.broadcasted_iota(jnp.int32, (block, tokens), 0) == target).astype(F32).astype(BF16)

    placer_own = placer_of(ids[...], c)
    pl.semaphore_wait(barrier, plane + 2)

    swap = [
        remote(ids, sibids, swap_s.at[0], swap_r.at[0], twin),
        remote(tok, sibx, swap_s.at[1], swap_r.at[1], twin),
        remote(gown, sibg, swap_s.at[2], swap_r.at[2], twin),
    ]
    for copy in swap:
        copy.start()
    load_in.start()
    load_out.start()
    swap[0].wait_recv()
    placer_sib = placer_of(sibids[...], o)

    own_src = (tok, gown)
    sib_src = (sibx, sibg)
    chunks = [(a, k) for a in range(2) for k in range(CHUNKS)]

    def place(q):
        a, k = chunks[q]
        placed = jnp.dot(placer_own, own_src[a][:, cols(k)], preferred_element_type=F32)
        placed += jnp.dot(placer_sib, sib_src[a][:, cols(k)], preferred_element_type=F32)
        stage[a, :, cols(k)] = placed.astype(BF16)

    def scatter(q):
        a, k = chunks[q]
        landing = XG.at[a, c, unit_rows(y * block + e * UNIT), cols(k)]
        pltpu.make_async_copy(stage.at[a, unit_rows(e * UNIT), cols(k)], landing, a2a_r.at[a, k]).start()

        def send(step, carry):
            to = (e + step) % plane
            remote(
                stage.at[a, unit_rows(to * UNIT), cols(k)], landing, a2a_s.at[a, k], a2a_r.at[a, k], dp, to
            ).start()
            return carry

        lax.fori_loop(1, plane, send, 0)

    ring_pieces = ((y_dn, 0), (y_dn, 1), (y_up, 0), (y_up, 1), (y_far, 0), (y_far, 1))

    def piece(q, f, where):
        a, k = chunks[q]
        return XG.at[a, f, block_rows(where[0]), part(k, where[1])]

    def to_twin(q, n, where):
        a, k = chunks[q]
        ref = piece(q, c, where)
        remote(ref, ref, sb_s.at[a, k, n], sb_r.at[a, k, n], twin).start()

    def send_own(q):
        a, k = chunks[q]
        wait_in(XG.at[a, c, block_rows(y), cols(k)], a2a_r.at[a, k])
        for h in range(2):
            for n, to in ((h, up), (2 + h, dn)):
                ref = piece(q, c, (y, h))
                remote(ref, ref, ag_s.at[a, k, n], ag_r.at[a, k, n], to).start()
        for h in range(2):
            to_twin(q, 6 + h, (y, h))

    def forward_on(q):
        a, k = chunks[q]
        for i, n, to in ((0, 4, up), (3, 5, dn)):
            ref = piece(q, c, ring_pieces[i])
            wait_in(ref, ag_r.at[a, k, i])
            remote(ref, ref, ag_s.at[a, k, n], ag_r.at[a, k, n], to).start()
            to_twin(q, i, ring_pieces[i])

    def take_rest(q):
        a, k = chunks[q]
        for i in (1, 2, 4, 5):
            wait_in(piece(q, c, ring_pieces[i]), ag_r.at[a, k, i])
            to_twin(q, i, ring_pieces[i])

    def wait_twin(a):
        for k in range(CHUNKS):
            q = a * CHUNKS + k
            for n, where in enumerate(ring_pieces + ((y, 0), (y, 1))):
                wait_in(piece(q, o, where), sb_r.at[a, k, n])

    def wait_gather_sends(a):
        for k in range(CHUNKS):
            q = a * CHUNKS + k
            for n in range(6):
                wait_out(piece(q, c, (y, 0)), ag_s.at[a, k, n])
            for n in range(8):
                wait_out(piece(q, c, (y, 0)), sb_s.at[a, k, n])

    def tile(t):
        return pl.ds(pl.multiple_of(t * tile_rows, tile_rows), tile_rows)

    def forward(f, t):
        rows = tile(t)
        pre = jnp.dot(X[f, rows, :], win[f], preferred_element_type=F32)
        cdf = 0.5 * (1.0 + lax.erf(pre * root_half))
        hid = (pre * cdf).astype(BF16)
        H[f, rows, :] = hid
        S[f, rows, :] = (cdf + pre * jnp.exp(-0.5 * pre * pre) * inv_root_tau).astype(BF16)
        for k in range(CHUNKS):
            Pf[f, rows, cols(k)] = jnp.dot(hid, wout[f, :, cols(k)], preferred_element_type=F32).astype(BF16)

    sums = (Pf, G)

    def partial_to_twin(d, k):
        remote(sums[d].at[o, :, cols(k)], sib.at[:, cols(k)], ps_s.at[d, k], ps_r.at[d, k], twin).start()

    def wait_partial_sends(d):
        for k in range(CHUNKS):
            wait_out(sib.at[:, cols(k)], ps_s.at[d, k])

    def rs_send(d, k, i, where, to):
        ref = sums[d].at[c, block_rows(where[0]), part(k, where[1])]
        remote(ref, rs.at[d, k, i], rs_s.at[d, k, i], rs_r.at[d, k, i], to).start()

    def add_twin(d, k, yb):
        rows = block_rows(yb)
        sums[d][c, rows, cols(k)] = (
            sums[d][c, rows, cols(k)].astype(F32) + sib[rows, cols(k)].astype(F32)
        ).astype(BF16)

    def add_ring(d, k, where, i):
        wait_in(rs.at[d, k, i], rs_r.at[d, k, i])
        rows, at = block_rows(where[0]), part(k, where[1])
        sums[d][c, rows, at] = (sums[d][c, rows, at].astype(F32) + rs[d, k, i].astype(F32)).astype(BF16)

    def reduce_start(d, k):
        wait_in(sib.at[:, cols(k)], ps_r.at[d, k])
        add_twin(d, k, y_far)
        rs_send(d, k, 0, (y_far, 0), up)
        rs_send(d, k, 3, (y_far, 1), dn)
        add_twin(d, k, y_up)
        rs_send(d, k, 1, (y_up, 1), up)
        add_twin(d, k, y_dn)
        rs_send(d, k, 4, (y_dn, 0), dn)
        add_twin(d, k, y)

    def reduce_middle(d, k):
        add_ring(d, k, (y_up, 0), 0)
        rs_send(d, k, 2, (y_up, 0), up)
        add_ring(d, k, (y_dn, 1), 3)
        rs_send(d, k, 5, (y_dn, 1), dn)

    def reduce_end(d, k):
        rows = block_rows(y)
        for h, ins in enumerate(((4, 2), (1, 5))):
            for i in ins:
                wait_in(rs.at[d, k, i], rs_r.at[d, k, i])
            at = part(k, h)
            sums[d][c, rows, at] = (
                sums[d][c, rows, at].astype(F32) + rs[d, k, ins[0]].astype(F32) + rs[d, k, ins[1]].astype(F32)
            ).astype(BF16)

        def leaving(to):
            return sums[d].at[c, unit_rows(y * block + to * UNIT), cols(k)]

        landing = aback.at[d, unit_rows(e * UNIT), cols(k)]
        pltpu.make_async_copy(leaving(e), landing, bk_r.at[d, k]).start()

        def send(step, carry):
            to = (e + step) % plane
            remote(leaving(to), landing, bk_s.at[d, k], bk_r.at[d, k], dp, to).start()
            return carry

        lax.fori_loop(1, plane, send, 0)

    kept = (mixed, tgrad)
    other_sum = (sibx, sibg)

    def unplace(d, k):
        wait_in(aback.at[d, :, cols(k)], bk_r.at[d, k])
        routed = aback[d, :, cols(k)]
        dims = (((0,), (0,)), ((), ()))
        leave = stage.at[d, pl.ds(0, tokens), cols(k)]
        leave[...] = lax.dot_general(placer_sib, routed, dims, preferred_element_type=F32).astype(BF16)
        remote(leave, other_sum[d].at[:, cols(k)], fn_s.at[d, k], fn_r.at[d, k], twin).start()
        kept[d][:, cols(k)] = lax.dot_general(placer_own, routed, dims, preferred_element_type=F32).astype(BF16)

    def token_rows(d, k):
        wait_in(other_sum[d].at[:, cols(k)], fn_r.at[d, k])
        return kept[d][:, cols(k)].astype(F32) + other_sum[d][:, cols(k)].astype(F32)

    transposed = (((1,), (1,)), ((), ()))
    over_rows = (((0,), (0,)), ((), ()))

    def hidden_back(f):
        def step(t, carry):
            rows = tile(t)
            back = lax.dot_general(G[f, rows, :], wout[f], transposed, preferred_element_type=F32)
            H[f, rows, :] = (back * S[f, rows, :].astype(F32)).astype(BF16)
            return carry

        lax.fori_loop(0, 2, step, 0)

    def token_back(f, k):
        def step(t, carry):
            rows = tile(t)
            G[f, rows, cols(k)] = lax.dot_general(
                H[f, rows, :], win[f, cols(k), :], transposed, preferred_element_type=F32
            ).astype(BF16)
            return carry

        lax.fori_loop(0, 2, step, 0)

    def out_tiles(f):
        def step(n, carry):
            at = pl.ds(pl.multiple_of(n * quarter, quarter), quarter)
            Pf[o, pl.ds(pl.multiple_of(f * hidden_width, hidden_width), hidden_width), at] = lax.dot_general(
                H[f], G[f, :, at], over_rows, preferred_element_type=F32
            ).astype(BF16)
            return carry

        lax.fori_loop(0, CHUNKS, step, 0)

    def in_weights_spot(f, m):
        return (
            o,
            pl.ds(pl.multiple_of(f * quarter, quarter), quarter),
            pl.ds(pl.multiple_of(m * hidden_width, hidden_width), hidden_width),
        )

    def in_copy(f, m):
        return pltpu.make_async_copy(
            Pf.at[in_weights_spot(f, m)], dwin_h.at[f, pl.ds(m * quarter, quarter)], out_s.at[2 + CHUNKS * f + m]
        )

    def in_tiles(f):
        def step(m, carry):
            at = pl.ds(pl.multiple_of(m * quarter, quarter), quarter)
            Pf[in_weights_spot(f, m)] = lax.dot_general(
                X[f, :, at], H[f], over_rows, preferred_element_type=F32
            ).astype(BF16)
            return carry

        lax.fori_loop(0, CHUNKS, step, 0)
        for m in range(CHUNKS):
            in_copy(f, m).start()

    swap[1].wait_recv()
    place(0)
    scatter(0)
    place(1)
    send_own(0)
    scatter(1)
    swap[2].wait_recv()
    place(2)
    place(3)
    send_own(1)
    scatter(2)
    forward_on(0)
    scatter(3)
    take_rest(0)
    place(4)
    place(5)
    send_own(2)
    forward_on(1)
    take_rest(1)
    scatter(4)
    send_own(3)
    forward_on(2)
    take_rest(2)
    scatter(5)
    place(6)
    place(7)
    send_own(4)
    scatter(6)
    forward_on(3)
    take_rest(3)
    send_own(5)
    scatter(7)
    load_in.wait()
    load_out.wait()
    wait_twin(0)
    send_own(6)
    forward(o, 0)
    forward_on(4)
    send_own(7)
    take_rest(4)
    forward(o, 1)
    for k in range(CHUNKS):
        partial_to_twin(0, k)
    forward_on(5)
    take_rest(5)
    forward_on(6)
    forward(c, 0)
    take_rest(6)
    forward_on(7)
    forward(c, 1)

    reduce_start(0, 0)
    reduce_start(0, 1)
    take_rest(7)
    wait_partial_sends(0)
    wait_twin(1)
    out_tiles(o)
    reduce_middle(0, 0)
    out_tiles(c)
    out_copies = [
        pltpu.make_async_copy(Pf.at[o, pl.ds(f * hidden_width, hidden_width)], dwout_h.at[f], out_s.at[f])
        for f in range(2)
    ]
    for copy in out_copies:
        copy.start()
    reduce_start(0, 2)
    reduce_middle(0, 1)
    hidden_back(o)
    reduce_start(0, 3)
    pl.semaphore_signal(credit, inc=1, device_id=(twin, e), device_id_type=MESH)
    reduce_end(0, 0)
    reduce_middle(0, 2)
    hidden_back(c)
    wait_gather_sends(1)
    pl.semaphore_wait(credit, 1)
    token_back(o, 0)
    partial_to_twin(1, 0)
    token_back(c, 0)
    token_back(o, 1)
    partial_to_twin(1, 1)
    token_back(c, 1)
    reduce_end(0, 1)
    reduce_middle(0, 3)
    reduce_start(1, 0)
    token_back(o, 2)
    partial_to_twin(1, 2)
    token_back(c, 2)
    token_back(o, 3)
    partial_to_twin(1, 3)
    token_back(c, 3)
    reduce_start(1, 1)
    reduce_end(0, 2)
    reduce_middle(1, 0)
    reduce_end(0, 3)

    sent_rows = UNIT * (plane - 1)
    for a in range(2):
        for k in range(CHUNKS):
            wait_out(stage.at[a, pl.ds(0, sent_rows), cols(k)], a2a_s.at[a, k])
    for copy in swap:
        copy.wait_send()
    for copy in out_copies:
        copy.wait()
    unplace(0, 0)
    unplace(0, 1)
    reduce_start(1, 2)
    reduce_middle(1, 1)
    in_tiles(0)
    reduce_start(1, 3)
    reduce_end(1, 0)
    reduce_middle(1, 2)
    in_tiles(1)
    unplace(0, 2)
    unplace(0, 3)
    reduce_end(1, 1)
    reduce_middle(1, 3)
    unplace(1, 0)
    gate_total = jnp.zeros((tokens, 1), F32)
    for k in range(CHUNKS):
        out_rows = token_rows(0, k)
        gate_total += jnp.sum(cot[:, cols(k)].astype(F32) * out_rows, 1, keepdims=True)
        mixed[:, cols(k)] = (gate_col * out_rows).astype(BF16)
    ggrad[...] = jnp.sum(jnp.where(diagonal, gate_total, 0.0), 0, keepdims=True)
    reduce_end(1, 2)
    unplace(1, 1)
    reduce_end(1, 3)
    unplace(1, 2)
    unplace(1, 3)
    for k in range(CHUNKS):
        tgrad[:, cols(k)] = token_rows(1, k).astype(BF16)

    wait_gather_sends(0)
    wait_partial_sends(1)
    for f in range(2):
        for m in range(CHUNKS):
            in_copy(f, m).wait()
    for d in range(2):
        for k in range(CHUNKS):
            for i in range(6):
                wait_out(rs.at[d, k, i], rs_s.at[d, k, i])
            wait_out(aback.at[d, pl.ds(0, sent_rows), cols(k)], bk_s.at[d, k])
            wait_out(stage.at[d, pl.ds(0, tokens), cols(k)], fn_s.at[d, k])


def hand_over_kernel(*refs):
    sources, targets, held, sems_in, sems_out = refs[:5], refs[5:10], refs[10:15], refs[15], refs[16]
    pieces = []
    for source, target, mid in zip(sources, targets, held):
        if len(source.shape) == 3:
            half = source.shape[1] // 2
            for f in range(source.shape[0]):
                for n in range(2):
                    at = (f, pl.ds(n * half, half))
                    pieces.append((source.at[at], mid.at[at], target.at[at]))
        else:
            pieces.append((source, mid, target))
    ins = [pltpu.make_async_copy(s, m, sems_in.at[n]) for n, (s, m, t) in enumerate(pieces)]
    outs = [pltpu.make_async_copy(m, t, sems_out.at[n]) for n, (s, m, t) in enumerate(pieces)]
    for copy in ins:
        copy.start()
    for arrived, leaving in zip(ins, outs):
        arrived.wait()
        leaving.start()
    for copy in outs:
        copy.wait()


def local(tokens, expert_ids, gate_weights, in_weights, out_weights, cotangent):
    plane = lax.axis_size("expert")
    count, features = tokens.shape
    hidden_width = in_weights.shape[2]
    block = UNIT * plane
    rows_all = NY * block
    vmem = pl.BlockSpec(memory_space=pltpu.VMEM)
    hbm = pl.BlockSpec(memory_space=pl.ANY)
    dma = pltpu.SemaphoreType.DMA
    shapes = (
        jax.ShapeDtypeStruct((count, features), BF16),
        jax.ShapeDtypeStruct((1, count), F32),
        jax.ShapeDtypeStruct((count, features), BF16),
        jax.ShapeDtypeStruct(in_weights.shape, BF16),
        jax.ShapeDtypeStruct(out_weights.shape, BF16),
    )
    results = pl.pallas_call(
        functools.partial(layer_kernel, plane),
        out_shape=shapes,
        in_specs=[vmem, vmem, vmem, vmem, hbm, hbm],
        out_specs=(vmem, vmem, vmem, hbm, hbm),
        scratch_shapes=[
            pltpu.VMEM((2, 2, rows_all, features), BF16),
            pltpu.VMEM(in_weights.shape, BF16),
            pltpu.VMEM(out_weights.shape, BF16),
            pltpu.VMEM((2, rows_all, hidden_width), BF16),
            pltpu.VMEM((2, rows_all, hidden_width), BF16),
            pltpu.VMEM((2, rows_all, features), BF16),
            pltpu.VMEM((rows_all, features), BF16),
            pltpu.VMEM((2, CHUNKS, 6, block, features // CHUNKS // 2), BF16),
            pltpu.VMEM((2, block, features), BF16),
            pltpu.VMEM((2, block, features), BF16),
            pltpu.VMEM((count, features), BF16),
            pltpu.VMEM((count, features), BF16),
            pltpu.VMEM((count, features), BF16),
            pltpu.VMEM((1, count), jnp.int32),
            dma((3,)), dma((3,)), dma((2,)),
            dma((2, CHUNKS)), dma((2, CHUNKS)),
            dma((2, CHUNKS, 6)), dma((2, CHUNKS, 6)),
            dma((2, CHUNKS, 8)), dma((2, CHUNKS, 8)),
            dma((2, CHUNKS)), dma((2, CHUNKS)),
            dma((2, CHUNKS, 6)), dma((2, CHUNKS, 6)),
            dma((2, CHUNKS)), dma((2, CHUNKS)),
            dma((2, CHUNKS)), dma((2, CHUNKS)),
            dma((2 + 2 * CHUNKS,)),
            pltpu.SemaphoreType.REGULAR,
        ],
        compiler_params=pltpu.CompilerParams(
            collective_id=0, has_side_effects=True, vmem_limit_bytes=60 * 1024 * 1024
        ),
    )(
        tokens, cotangent, gate_weights.reshape(1, count), expert_ids.reshape(1, count), in_weights, out_weights,
    )
    mixed, gate_grad, token_grad, in_grad, out_grad = pl.pallas_call(
        hand_over_kernel,
        out_shape=shapes,
        in_specs=[pl.BlockSpec(memory_space=pltpu.HBM)] * 5,
        out_specs=(pl.BlockSpec(memory_space=pltpu.HBM),) * 5,
        scratch_shapes=[pltpu.VMEM(shape.shape, shape.dtype) for shape in shapes] + [dma((11,)), dma((11,))],
        compiler_params=pltpu.CompilerParams(vmem_limit_bytes=60 * 1024 * 1024),
    )(*results)
    return mixed, gate_grad.reshape(count), token_grad, in_grad, out_grad


def solution(mesh):
    in_specs = (
        P(("dp", "expert"), None),
        P(("dp", "expert")),
        P(("dp", "expert")),
        P("expert", None, "dp"),
        P("expert", "dp", None),
        P(("dp", "expert"), None),
    )
    out_specs = (
        P(("dp", "expert"), None),
        P(("dp", "expert")),
        P(("dp", "expert"), None),
        P("expert", None, "dp"),
        P("expert", "dp", None),
    )
    return jax.shard_map(local, mesh=mesh, in_specs=in_specs, out_specs=out_specs, check_vma=False)
```

```python
import functools

import jax
import jax.numpy as jnp
from jax import lax
from jax.experimental import pallas as pl
from jax.experimental.pallas import tpu as pltpu
from jax.sharding import PartitionSpec as P

root_half = 0.7071067811865476
inv_root_tau = 0.3989422804014327
MESH = pl.DeviceIdType.MESH
CAP = 8
UNIT = 2 * CAP
NY = 4
CHUNKS = 4
LAST = CHUNKS - 1
BF16, F32 = jnp.bfloat16, jnp.float32


def layer_kernel(
    plane,
    tok, cot, gate, ids, win_h, wout_h,
    mixed, ggrad, tgrad, dwin_h, dwout_h,
    XG, win, wout, S, H, Pf, sib, rs, rs_raw, stage, aback, aback_all, gown, sibx, sibg, all_ids, placers,
    swap_s, swap_r, w_s, a2a_s, a2a_r, ag_s, ag_r, sb_s, sb_r, ps_s, ps_r, rs_s, rs_r,
    bk_s, bk_r, fn_s, fn_r, out_s, ids_s, ids_r, raw_s, raw_r, rt_s, rt_r, ab_s, ab_r, bb_s, bb_r, ft_s, ft_r, credit,
):
    tokens, features = tok.shape
    block = UNIT * plane
    rows_all = NY * block
    hidden_width = win.shape[2]
    tile_rows = rows_all // 2
    quarter = features // CHUNKS
    eighth = quarter // 2
    X, G = XG.at[0], XG.at[1]

    dp = lax.axis_index("dp")
    e = lax.axis_index("expert")
    y = dp // 2
    c = dp % 2
    o = 1 - c
    y_up, y_dn, y_far = (y + 1) % NY, (y + 3) % NY, (y + 2) % NY
    up, dn, twin = y_up * 2 + c, y_dn * 2 + c, y * 2 + o

    def remote(src, dst, ssem, rsem, to_dp, to_e=None):
        return pltpu.make_async_remote_copy(
            src_ref=src, dst_ref=dst, send_sem=ssem, recv_sem=rsem,
            device_id=(to_dp, e if to_e is None else to_e), device_id_type=MESH,
        )

    def wait_in(ref, sem):
        remote(ref, ref, sem, sem, dp).wait_recv()

    def wait_out(ref, sem):
        remote(ref, ref, sem, sem, dp).wait_send()

    def cols(k):
        return pl.ds(k * quarter, quarter)

    def part(k, h):
        return pl.ds(k * quarter + h * eighth, eighth)

    def block_rows(yb):
        return pl.ds(pl.multiple_of(yb * block, block), block)

    def unit_rows(start):
        return pl.ds(pl.multiple_of(start, UNIT), UNIT)

    load_in = pltpu.make_async_copy(win_h, win, w_s.at[0])
    load_out = pltpu.make_async_copy(wout_h, wout, w_s.at[1])

    barrier = pltpu.get_barrier_semaphore()

    def greet(k, carry):
        pl.semaphore_signal(barrier, inc=1, device_id=(dp, (e + k) % plane), device_id_type=MESH)
        return carry

    def greet_dp(k, carry):
        pl.semaphore_signal(barrier, inc=1, device_id=((dp + k) % (2 * NY), e), device_id_type=MESH)
        return carry

    lax.fori_loop(1, 2 * NY, greet_dp, 0)
    lax.fori_loop(1, plane, greet, 0)

    diagonal = lax.broadcasted_iota(jnp.int32, (tokens, tokens), 0) == lax.broadcasted_iota(
        jnp.int32, (tokens, tokens), 1
    )
    gate_col = jnp.sum(jnp.where(diagonal, gate[...], 0.0), 1, keepdims=True)
    gown[...] = (gate_col * cot[...].astype(F32)).astype(BF16)

    def placer_of(id_row, core):
        n_experts = 2 * plane
        onehot = lax.broadcasted_iota(jnp.int32, (n_experts, tokens), 0) == id_row
        onehot_f = onehot.astype(F32)
        before = (
            lax.broadcasted_iota(jnp.int32, (tokens, tokens), 0)
            < lax.broadcasted_iota(jnp.int32, (tokens, tokens), 1)
        ).astype(F32).astype(BF16)
        rank = jnp.dot(onehot_f.astype(BF16), before, preferred_element_type=F32)
        slot = jnp.sum(rank * onehot_f, 0, keepdims=True).astype(jnp.int32)
        target = (id_row >> 1) * UNIT + core * CAP + slot
        target = jnp.where((id_row & 1) == c, target, -1)
        return (lax.broadcasted_iota(jnp.int32, (block, tokens), 0) == target).astype(F32).astype(BF16)

    placers[0, y] = placer_of(ids[...], c)
    pl.semaphore_wait(barrier, plane - 1 + 2 * NY - 1)

    for k in range(1, 2 * NY):
        remote(ids, all_ids.at[dp], ids_s.at[k], ids_r.at[k], (dp + k) % (2 * NY)).start()
    swap = [
        remote(tok, sibx, swap_s.at[0], swap_r.at[0], twin),
        remote(gown, sibg, swap_s.at[1], swap_r.at[1], twin),
    ]

    own_src = (tok, gown)
    sib_src = (sibx, sibg)
    chunks = [(a, k) for a in range(2) for k in range(CHUNKS)]

    blocks_y = (y, y_up, y_dn, y_far)

    def raw_rows(core, yb):
        return pl.ds(pl.multiple_of((core * NY + yb) * tokens, tokens), tokens)

    def raw_at(a, core, yb, h):
        return Pf.at[a, raw_rows(core, yb), pl.ds(h * eighth, eighth)]

    def raw_own(a):
        for h in range(2):
            for n, to in ((h, up), (2 + h, dn)):
                remote(
                    own_src[a].at[:, part(LAST, h)], raw_at(a, c, y, h), raw_s.at[a, n], raw_r.at[a, n], to
                ).start()

    def raw_to_twin(a, i):
        yb, h = raw_pieces[i]
        ref = raw_at(a, c, yb, h)
        remote(ref, ref, rt_s.at[a, i], rt_r.at[a, i], twin).start()

    raw_pieces = ((y_dn, 0), (y_dn, 1), (y_up, 0), (y_up, 1), (y_far, 0), (y_far, 1))

    def raw_forward(a):
        for i, n, to in ((0, 4, up), (3, 5, dn)):
            ref = raw_at(a, c, *raw_pieces[i])
            wait_in(ref, raw_r.at[a, i])
            remote(ref, ref, raw_s.at[a, n], raw_r.at[a, n], to).start()
            raw_to_twin(a, i)

    def raw_rest(a):
        for i in (1, 2, 4, 5):
            wait_in(raw_at(a, c, *raw_pieces[i]), raw_r.at[a, i])
            raw_to_twin(a, i)

    def raw_wait_twin(a):
        for i in range(6):
            wait_in(raw_at(a, o, *raw_pieces[i]), rt_r.at[a, i])

    def raw_wait_sends(a):
        for i in range(6):
            wait_out(raw_at(a, c, y, 0), raw_s.at[a, i])
            wait_out(raw_at(a, c, y, 0), rt_s.at[a, i])

    def wide_stage(a, yb):
        if a == 0:
            return Pf.at[0, block_rows(yb), pl.ds(quarter, quarter)]
        return sib.at[block_rows(yb), pl.ds(0, quarter)]

    def wide_place(a):
        for j, yb in enumerate(blocks_y):
            if j == 0:
                mine, theirs = own_src[a][:, cols(LAST)], sib_src[a][:, cols(LAST)]
            else:
                mine = Pf[a, raw_rows(c, yb), pl.ds(0, quarter)]
                theirs = Pf[a, raw_rows(o, yb), pl.ds(0, quarter)]
            placed = jnp.dot(placers[0, yb], mine, preferred_element_type=F32)
            placed += jnp.dot(placers[1, yb], theirs, preferred_element_type=F32)
            wide_stage(a, yb)[...] = placed.astype(BF16)

    def wide_scatter(a, j):
        yb = blocks_y[j]
        landing = XG.at[a, c, unit_rows(yb * block + e * UNIT), cols(LAST)]
        source = wide_stage(a, yb)
        pltpu.make_async_copy(source.at[unit_rows(e * UNIT)], landing, ab_r.at[a, j]).start()

        def send(step, carry):
            to = (e + step) % plane
            remote(source.at[unit_rows(to * UNIT)], landing, ab_s.at[a, j], ab_r.at[a, j], dp, to).start()
            return carry

        lax.fori_loop(1, plane, send, 0)

    def wide_wait_sends(a):
        for j in range(NY):
            wait_out(wide_stage(a, y).at[pl.ds(0, UNIT * (plane - 1))], ab_s.at[a, j])

    def wide_arrived(a, j):
        ref = XG.at[a, c, block_rows(blocks_y[j]), cols(LAST)]
        wait_in(ref, ab_r.at[a, j])
        remote(ref, ref, sb_s.at[a, LAST, j], sb_r.at[a, LAST, j], twin).start()

    def place(q):
        a, k = chunks[q]
        placed = jnp.dot(placers[0, y], own_src[a][:, cols(k)], preferred_element_type=F32)
        placed += jnp.dot(placers[1, y], sib_src[a][:, cols(k)], preferred_element_type=F32)
        stage[a, :, cols(k)] = placed.astype(BF16)

    def scatter(q):
        a, k = chunks[q]
        landing = XG.at[a, c, unit_rows(y * block + e * UNIT), cols(k)]
        pltpu.make_async_copy(stage.at[a, unit_rows(e * UNIT), cols(k)], landing, a2a_r.at[a, k]).start()

        def send(step, carry):
            to = (e + step) % plane
            remote(
                stage.at[a, unit_rows(to * UNIT), cols(k)], landing, a2a_s.at[a, k], a2a_r.at[a, k], dp, to
            ).start()
            return carry

        lax.fori_loop(1, plane, send, 0)

    ring_pieces = ((y_dn, 0), (y_dn, 1), (y_up, 0), (y_up, 1), (y_far, 0), (y_far, 1))

    def piece(q, f, where):
        a, k = chunks[q]
        return XG.at[a, f, block_rows(where[0]), part(k, where[1])]

    def to_twin(q, n, where):
        a, k = chunks[q]
        ref = piece(q, c, where)
        remote(ref, ref, sb_s.at[a, k, n], sb_r.at[a, k, n], twin).start()

    def send_own(q):
        a, k = chunks[q]
        wait_in(XG.at[a, c, block_rows(y), cols(k)], a2a_r.at[a, k])
        for h in range(2):
            for n, to in ((h, up), (2 + h, dn)):
                ref = piece(q, c, (y, h))
                remote(ref, ref, ag_s.at[a, k, n], ag_r.at[a, k, n], to).start()
        for h in range(2):
            to_twin(q, 6 + h, (y, h))

    def forward_on(q):
        a, k = chunks[q]
        for i, n, to in ((0, 4, up), (3, 5, dn)):
            ref = piece(q, c, ring_pieces[i])
            wait_in(ref, ag_r.at[a, k, i])
            remote(ref, ref, ag_s.at[a, k, n], ag_r.at[a, k, n], to).start()
            to_twin(q, i, ring_pieces[i])

    def take_rest(q):
        a, k = chunks[q]
        for i in (1, 2, 4, 5):
            wait_in(piece(q, c, ring_pieces[i]), ag_r.at[a, k, i])
            to_twin(q, i, ring_pieces[i])

    def wait_twin(a):
        for j in range(NY):
            wait_in(XG.at[a, o, block_rows(blocks_y[j]), cols(LAST)], sb_r.at[a, LAST, j])
        for k in range(LAST):
            q = a * CHUNKS + k
            for n, where in enumerate(ring_pieces + ((y, 0), (y, 1))):
                wait_in(piece(q, o, where), sb_r.at[a, k, n])

    def wait_gather_sends(a):
        for j in range(NY):
            wait_out(XG.at[a, c, block_rows(y), cols(LAST)], sb_s.at[a, LAST, j])
        for k in range(LAST):
            q = a * CHUNKS + k
            for n in range(6):
                wait_out(piece(q, c, (y, 0)), ag_s.at[a, k, n])
            for n in range(8):
                wait_out(piece(q, c, (y, 0)), sb_s.at[a, k, n])

    def tile(t):
        return pl.ds(pl.multiple_of(t * tile_rows, tile_rows), tile_rows)

    def forward(f, t):
        rows = tile(t)
        pre = jnp.dot(X[f, rows, :], win[f], preferred_element_type=F32)
        cdf = 0.5 * (1.0 + lax.erf(pre * root_half))
        hid = (pre * cdf).astype(BF16)
        H[f, rows, :] = hid
        S[f, rows, :] = (cdf + pre * jnp.exp(-0.5 * pre * pre) * inv_root_tau).astype(BF16)
        for k in range(CHUNKS):
            Pf[f, rows, cols(k)] = jnp.dot(hid, wout[f, :, cols(k)], preferred_element_type=F32).astype(BF16)

    sums = (Pf, G)

    def partial_to_twin(d, k):
        remote(sums[d].at[o, :, cols(k)], sib.at[:, cols(k)], ps_s.at[d, k], ps_r.at[d, k], twin).start()

    def wait_partial_sends(d):
        for k in range(CHUNKS):
            wait_out(sib.at[:, cols(k)], ps_s.at[d, k])

    def rs_send(d, k, i, where, to):
        ref = sums[d].at[c, block_rows(where[0]), part(k, where[1])]
        remote(ref, rs.at[d, k, i], rs_s.at[d, k, i], rs_r.at[d, k, i], to).start()

    def add_twin(d, k, yb):
        rows = block_rows(yb)
        sums[d][c, rows, cols(k)] = (
            sums[d][c, rows, cols(k)].astype(F32) + sib[rows, cols(k)].astype(F32)
        ).astype(BF16)

    def add_ring(d, k, where, i):
        wait_in(rs.at[d, k, i], rs_r.at[d, k, i])
        rows, at = block_rows(where[0]), part(k, where[1])
        sums[d][c, rows, at] = (sums[d][c, rows, at].astype(F32) + rs[d, k, i].astype(F32)).astype(BF16)

    def reduce_start(d, k):
        wait_in(sib.at[:, cols(k)], ps_r.at[d, k])
        add_twin(d, k, y_far)
        rs_send(d, k, 0, (y_far, 0), up)
        rs_send(d, k, 3, (y_far, 1), dn)
        add_twin(d, k, y_up)
        rs_send(d, k, 1, (y_up, 1), up)
        add_twin(d, k, y_dn)
        rs_send(d, k, 4, (y_dn, 0), dn)
        add_twin(d, k, y)

    def reduce_middle(d, k):
        add_ring(d, k, (y_up, 0), 0)
        rs_send(d, k, 2, (y_up, 0), up)
        add_ring(d, k, (y_dn, 1), 3)
        rs_send(d, k, 5, (y_dn, 1), dn)

    def reduce_end(d, k):
        rows = block_rows(y)
        for h, ins in enumerate(((4, 2), (1, 5))):
            for i in ins:
                wait_in(rs.at[d, k, i], rs_r.at[d, k, i])
            at = part(k, h)
            sums[d][c, rows, at] = (
                sums[d][c, rows, at].astype(F32) + rs[d, k, ins[0]].astype(F32) + rs[d, k, ins[1]].astype(F32)
            ).astype(BF16)

        def leaving(to):
            return sums[d].at[c, unit_rows(y * block + to * UNIT), cols(k)]

        landing = aback.at[d, unit_rows(e * UNIT), cols(k)]
        pltpu.make_async_copy(leaving(e), landing, bk_r.at[d, k]).start()

        def send(step, carry):
            to = (e + step) % plane
            remote(leaving(to), landing, bk_s.at[d, k], bk_r.at[d, k], dp, to).start()
            return carry

        lax.fori_loop(1, plane, send, 0)

    kept = (mixed, tgrad)
    other_sum = (sibx, sibg)

    def unplace(d, k):
        wait_in(aback.at[d, :, cols(k)], bk_r.at[d, k])
        routed = aback[d, :, cols(k)]
        dims = (((0,), (0,)), ((), ()))
        leave = stage.at[d, pl.ds(0, tokens), cols(k)]
        leave[...] = lax.dot_general(placers[1, y], routed, dims, preferred_element_type=F32).astype(BF16)
        remote(leave, other_sum[d].at[:, cols(k)], fn_s.at[d, k], fn_r.at[d, k], twin).start()
        kept[d][:, cols(k)] = lax.dot_general(placers[0, y], routed, dims, preferred_element_type=F32).astype(BF16)

    def wide_leave(d):
        wait_in(sib.at[:, cols(LAST)], ps_r.at[d, LAST])
        for j, yb in enumerate(blocks_y):
            add_twin(d, LAST, yb)
            landing = aback_all.at[d, yb, unit_rows(e * UNIT)]
            source = sums[d].at[c, block_rows(yb), cols(LAST)]
            pltpu.make_async_copy(source.at[unit_rows(e * UNIT)], landing, bb_r.at[d, j]).start()

            def send(step, carry, j=j, landing=landing, source=source):
                to = (e + step) % plane
                remote(source.at[unit_rows(to * UNIT)], landing, bb_s.at[d, j], bb_r.at[d, j], dp, to).start()
                return carry

            lax.fori_loop(1, plane, send, 0)

    def raw_in(d, yb):
        return S.at[d, pl.ds(pl.multiple_of(yb * tokens, tokens), tokens), pl.ds(0, quarter)]

    def wide_unplace(d):
        dims = (((0,), (0,)), ((), ()))
        for j, yb in enumerate(blocks_y):
            wait_in(aback_all.at[d, yb], bb_r.at[d, j])
            routed = aback_all[d, yb]
            mine = lax.dot_general(placers[0, yb], routed, dims, preferred_element_type=F32).astype(BF16)
            theirs = lax.dot_general(placers[1, yb], routed, dims, preferred_element_type=F32).astype(BF16)
            aback_all[d, yb, pl.ds(0, tokens)] = mine
            leave = aback_all.at[d, yb, pl.ds(tokens, tokens)]
            leave[...] = theirs
            remote(leave, raw_in(d, yb), ft_s.at[d, j], ft_r.at[d, j], twin).start()

    def raw_total(d, where):
        return aback_all.at[d, where[0], pl.ds(0, tokens), pl.ds(where[1] * eighth, eighth)]

    def raw_send(d, i, where, to):
        remote(raw_total(d, where), rs_raw.at[d, i], rs_s.at[d, LAST, i], rs_r.at[d, LAST, i], to).start()

    def raw_add(d, where, i):
        wait_in(rs_raw.at[d, i], rs_r.at[d, LAST, i])
        ref = raw_total(d, where)
        ref[...] = (ref[...].astype(F32) + rs_raw[d, i].astype(F32)).astype(BF16)

    def raw_sum_start(d):
        for j in (3, 1, 2, 0):
            yb = blocks_y[j]
            wait_in(raw_in(d, yb), ft_r.at[d, j])
            own = aback_all.at[d, yb, pl.ds(0, tokens)]
            own[...] = (own[...].astype(F32) + raw_in(d, yb)[...].astype(F32)).astype(BF16)
        raw_send(d, 0, (y_far, 0), up)
        raw_send(d, 3, (y_far, 1), dn)
        raw_send(d, 1, (y_up, 1), up)
        raw_send(d, 4, (y_dn, 0), dn)

    def raw_sum_middle(d):
        raw_add(d, (y_up, 0), 0)
        raw_send(d, 2, (y_up, 0), up)
        raw_add(d, (y_dn, 1), 3)
        raw_send(d, 5, (y_dn, 1), dn)

    def raw_sum_end(d):
        for h, ins in enumerate(((4, 2), (1, 5))):
            for i in ins:
                wait_in(rs_raw.at[d, i], rs_r.at[d, LAST, i])
            kept[d][:, part(LAST, h)] = (
                raw_total(d, (y, h))[...].astype(F32) + rs_raw[d, ins[0]].astype(F32) + rs_raw[d, ins[1]].astype(F32)
            ).astype(BF16)

    def token_rows(d, k):
        if k == LAST:
            return kept[d][:, cols(k)].astype(F32)
        wait_in(other_sum[d].at[:, cols(k)], fn_r.at[d, k])
        return kept[d][:, cols(k)].astype(F32) + other_sum[d][:, cols(k)].astype(F32)

    transposed = (((1,), (1,)), ((), ()))
    over_rows = (((0,), (0,)), ((), ()))

    def hidden_back(f):
        def step(t, carry):
            rows = tile(t)
            back = lax.dot_general(G[f, rows, :], wout[f], transposed, preferred_element_type=F32)
            H[f, rows, :] = (back * S[f, rows, :].astype(F32)).astype(BF16)
            return carry

        lax.fori_loop(0, 2, step, 0)

    def token_back(f, k):
        def step(t, carry):
            rows = tile(t)
            G[f, rows, cols(k)] = lax.dot_general(
                H[f, rows, :], win[f, cols(k), :], transposed, preferred_element_type=F32
            ).astype(BF16)
            return carry

        lax.fori_loop(0, 2, step, 0)

    def out_tiles(f):
        def step(n, carry):
            at = pl.ds(pl.multiple_of(n * quarter, quarter), quarter)
            Pf[o, pl.ds(pl.multiple_of(f * hidden_width, hidden_width), hidden_width), at] = lax.dot_general(
                H[f], G[f, :, at], over_rows, preferred_element_type=F32
            ).astype(BF16)
            return carry

        lax.fori_loop(0, CHUNKS, step, 0)

    def in_weights_spot(f, m):
        return (
            o,
            pl.ds(pl.multiple_of(f * quarter, quarter), quarter),
            pl.ds(pl.multiple_of(m * hidden_width, hidden_width), hidden_width),
        )

    def in_copy(f, m):
        return pltpu.make_async_copy(
            Pf.at[in_weights_spot(f, m)], dwin_h.at[f, pl.ds(m * quarter, quarter)], out_s.at[2 + CHUNKS * f + m]
        )

    def in_tiles(f):
        def step(m, carry):
            at = pl.ds(pl.multiple_of(m * quarter, quarter), quarter)
            Pf[in_weights_spot(f, m)] = lax.dot_general(
                X[f, :, at], H[f], over_rows, preferred_element_type=F32
            ).astype(BF16)
            return carry

        lax.fori_loop(0, CHUNKS, step, 0)
        for m in range(CHUNKS):
            in_copy(f, m).start()

    swap[0].start()
    raw_own(0)
    swap[1].start()
    raw_own(1)
    load_in.start()
    load_out.start()

    for k in range(1, 2 * NY):
        wait_in(all_ids.at[(dp + 2 * NY - k) % (2 * NY)], ids_r.at[k])
    placers[1, y] = placer_of(all_ids[twin], o)
    swap[0].wait_recv()
    place(0)
    scatter(0)
    for yb in (y_dn, y_up, y_far):
        placers[0, yb] = placer_of(all_ids[yb * 2 + c], c)
        placers[1, yb] = placer_of(all_ids[yb * 2 + o], o)
    raw_forward(0)
    place(1)
    send_own(0)
    scatter(1)
    raw_rest(0)
    raw_forward(1)
    place(2)
    send_own(1)
    scatter(2)
    forward_on(0)
    raw_wait_twin(0)
    wide_place(0)
    wide_scatter(0, 0)
    wide_scatter(0, 1)
    swap[1].wait_recv()
    place(4)
    place(5)
    place(6)
    take_rest(0)
    send_own(2)
    wide_scatter(0, 2)
    wide_scatter(0, 3)
    forward_on(1)
    raw_rest(1)
    raw_wait_twin(1)
    wide_place(1)
    scatter(4)
    take_rest(1)
    forward_on(2)
    wide_arrived(0, 0)
    wide_arrived(0, 1)
    send_own(4)
    scatter(5)
    wide_scatter(1, 0)
    take_rest(2)
    wide_arrived(0, 2)
    wide_arrived(0, 3)
    scatter(6)
    wide_scatter(1, 1)
    send_own(5)
    wide_scatter(1, 2)
    wide_scatter(1, 3)
    raw_wait_sends(0)
    raw_wait_sends(1)
    wide_wait_sends(0)
    load_in.wait()
    load_out.wait()
    wait_twin(0)
    forward(o, 0)
    forward_on(4)
    send_own(6)
    take_rest(4)
    forward_on(5)
    wide_arrived(1, 0)
    wide_arrived(1, 1)
    forward(o, 1)
    wide_arrived(1, 2)
    wide_arrived(1, 3)
    wide_wait_sends(1)
    pl.semaphore_signal(credit, inc=1, device_id=(twin, e), device_id_type=MESH)
    pl.semaphore_wait(credit, 1)
    for k in (LAST, 0, 1, 2):
        partial_to_twin(0, k)
    take_rest(5)
    forward_on(6)
    forward(c, 0)
    take_rest(6)
    forward(c, 1)

    reduce_start(0, 0)
    wide_leave(0)
    reduce_start(0, 1)
    wait_partial_sends(0)
    wait_twin(1)
    out_tiles(o)
    reduce_middle(0, 0)
    out_tiles(c)
    out_copies = [
        pltpu.make_async_copy(Pf.at[o, pl.ds(f * hidden_width, hidden_width)], dwout_h.at[f], out_s.at[f])
        for f in range(2)
    ]
    for copy in out_copies:
        copy.start()
    reduce_start(0, 2)
    pl.semaphore_signal(credit, inc=1, device_id=(twin, e), device_id_type=MESH)
    reduce_middle(0, 1)
    hidden_back(o)
    reduce_end(0, 0)
    hidden_back(c)
    wait_gather_sends(1)
    pl.semaphore_wait(credit, 1)
    token_back(o, LAST)
    partial_to_twin(1, LAST)
    token_back(c, LAST)
    reduce_middle(0, 2)
    token_back(o, 0)
    partial_to_twin(1, 0)
    token_back(c, 0)
    wide_leave(1)
    wide_unplace(0)
    reduce_start(1, 0)
    token_back(o, 1)
    partial_to_twin(1, 1)
    token_back(c, 1)
    reduce_end(0, 1)
    raw_sum_start(0)
    token_back(o, 2)
    partial_to_twin(1, 2)
    token_back(c, 2)
    reduce_start(1, 1)
    reduce_end(0, 2)
    reduce_middle(1, 0)
    raw_sum_middle(0)
    wide_unplace(1)
    raw_sum_start(1)

    sent_rows = UNIT * (plane - 1)
    for a in range(2):
        for k in range(LAST):
            wait_out(stage.at[a, pl.ds(0, sent_rows), cols(k)], a2a_s.at[a, k])
    for copy in swap:
        copy.wait_send()
    for copy in out_copies:
        copy.wait()
    unplace(0, 0)
    reduce_start(1, 2)
    reduce_middle(1, 1)
    raw_sum_middle(1)
    in_tiles(0)
    reduce_end(1, 0)
    unplace(0, 1)
    reduce_middle(1, 2)
    raw_sum_end(0)
    in_tiles(1)
    reduce_end(1, 1)
    unplace(0, 2)
    raw_sum_end(1)
    gate_total = jnp.zeros((tokens, 1), F32)
    for k in range(CHUNKS):
        out_rows = token_rows(0, k)
        gate_total += jnp.sum(cot[:, cols(k)].astype(F32) * out_rows, 1, keepdims=True)
        mixed[:, cols(k)] = (gate_col * out_rows).astype(BF16)
    ggrad[...] = jnp.sum(jnp.where(diagonal, gate_total, 0.0), 0, keepdims=True)
    unplace(1, 0)
    reduce_end(1, 2)
    unplace(1, 1)
    tgrad[:, cols(0)] = token_rows(1, 0).astype(BF16)
    tgrad[:, cols(1)] = token_rows(1, 1).astype(BF16)
    unplace(1, 2)
    tgrad[:, cols(2)] = token_rows(1, 2).astype(BF16)

    wait_gather_sends(0)
    wait_partial_sends(1)
    for f in range(2):
        for m in range(CHUNKS):
            in_copy(f, m).wait()
    for k in range(1, 2 * NY):
        wait_out(ids, ids_s.at[k])
    for d in range(2):
        for i in range(6):
            wait_out(rs_raw.at[d, i], rs_s.at[d, LAST, i])
        for j in range(NY):
            wait_out(aback_all.at[d, y, pl.ds(0, sent_rows)], bb_s.at[d, j])
            wait_out(raw_in(d, y), ft_s.at[d, j])
        for k in range(LAST):
            for i in range(6):
                wait_out(rs.at[d, k, i], rs_s.at[d, k, i])
            wait_out(aback.at[d, pl.ds(0, sent_rows), cols(k)], bk_s.at[d, k])
            wait_out(stage.at[d, pl.ds(0, tokens), cols(k)], fn_s.at[d, k])


def hand_over_kernel(*refs):
    sources, targets, held, sems_in, sems_out = refs[:5], refs[5:10], refs[10:15], refs[15], refs[16]
    pieces = []
    for source, target, mid in zip(sources, targets, held):
        if len(source.shape) == 3:
            half = source.shape[1] // 2
            for f in range(source.shape[0]):
                for n in range(2):
                    at = (f, pl.ds(n * half, half))
                    pieces.append((source.at[at], mid.at[at], target.at[at]))
        else:
            pieces.append((source, mid, target))
    ins = [pltpu.make_async_copy(s, m, sems_in.at[n]) for n, (s, m, t) in enumerate(pieces)]
    outs = [pltpu.make_async_copy(m, t, sems_out.at[n]) for n, (s, m, t) in enumerate(pieces)]
    for copy in ins:
        copy.start()
    for arrived, leaving in zip(ins, outs):
        arrived.wait()
        leaving.start()
    for copy in outs:
        copy.wait()


def local(tokens, expert_ids, gate_weights, in_weights, out_weights, cotangent):
    plane = lax.axis_size("expert")
    count, features = tokens.shape
    hidden_width = in_weights.shape[2]
    block = UNIT * plane
    rows_all = NY * block
    quarter = features // CHUNKS
    vmem = pl.BlockSpec(memory_space=pltpu.VMEM)
    hbm = pl.BlockSpec(memory_space=pl.ANY)
    dma = pltpu.SemaphoreType.DMA
    shapes = (
        jax.ShapeDtypeStruct((count, features), BF16),
        jax.ShapeDtypeStruct((1, count), F32),
        jax.ShapeDtypeStruct((count, features), BF16),
        jax.ShapeDtypeStruct(in_weights.shape, BF16),
        jax.ShapeDtypeStruct(out_weights.shape, BF16),
    )
    results = pl.pallas_call(
        functools.partial(layer_kernel, plane),
        out_shape=shapes,
        in_specs=[vmem, vmem, vmem, vmem, hbm, hbm],
        out_specs=(vmem, vmem, vmem, hbm, hbm),
        scratch_shapes=[
            pltpu.VMEM((2, 2, rows_all, features), BF16),
            pltpu.VMEM(in_weights.shape, BF16),
            pltpu.VMEM(out_weights.shape, BF16),
            pltpu.VMEM((2, rows_all, hidden_width), BF16),
            pltpu.VMEM((2, rows_all, hidden_width), BF16),
            pltpu.VMEM((2, rows_all, features), BF16),
            pltpu.VMEM((rows_all, features), BF16),
            pltpu.VMEM((2, LAST, 6, block, quarter // 2), BF16),
            pltpu.VMEM((2, 6, count, quarter // 2), BF16),
            pltpu.VMEM((2, block, LAST * quarter), BF16),
            pltpu.VMEM((2, block, LAST * quarter), BF16),
            pltpu.VMEM((2, NY, block, quarter), BF16),
            pltpu.VMEM((count, features), BF16),
            pltpu.VMEM((count, features), BF16),
            pltpu.VMEM((count, features), BF16),
            pltpu.VMEM((2 * NY, 1, count), jnp.int32),
            pltpu.VMEM((2, NY, block, count), BF16),
            dma((2,)), dma((2,)), dma((2,)),
            dma((2, CHUNKS)), dma((2, CHUNKS)),
            dma((2, CHUNKS, 6)), dma((2, CHUNKS, 6)),
            dma((2, CHUNKS, 8)), dma((2, CHUNKS, 8)),
            dma((2, CHUNKS)), dma((2, CHUNKS)),
            dma((2, CHUNKS, 6)), dma((2, CHUNKS, 6)),
            dma((2, CHUNKS)), dma((2, CHUNKS)),
            dma((2, CHUNKS)), dma((2, CHUNKS)),
            dma((2 + 2 * CHUNKS,)),
            dma((2 * NY,)), dma((2 * NY,)),
            dma((2, 6)), dma((2, 6)),
            dma((2, 6)), dma((2, 6)),
            dma((2, NY)), dma((2, NY)),
            dma((2, NY)), dma((2, NY)),
            dma((2, NY)), dma((2, NY)),
            pltpu.SemaphoreType.REGULAR,
        ],
        compiler_params=pltpu.CompilerParams(
            collective_id=0, has_side_effects=True, vmem_limit_bytes=60 * 1024 * 1024
        ),
    )(
        tokens, cotangent, gate_weights.reshape(1, count), expert_ids.reshape(1, count), in_weights, out_weights,
    )
    mixed, gate_grad, token_grad, in_grad, out_grad = pl.pallas_call(
        hand_over_kernel,
        out_shape=shapes,
        in_specs=[pl.BlockSpec(memory_space=pltpu.HBM)] * 5,
        out_specs=(pl.BlockSpec(memory_space=pltpu.HBM),) * 5,
        scratch_shapes=[pltpu.VMEM(shape.shape, shape.dtype) for shape in shapes] + [dma((11,)), dma((11,))],
        compiler_params=pltpu.CompilerParams(vmem_limit_bytes=60 * 1024 * 1024),
    )(*results)
    return mixed, gate_grad.reshape(count), token_grad, in_grad, out_grad


def solution(mesh):
    in_specs = (
        P(("dp", "expert"), None),
        P(("dp", "expert")),
        P(("dp", "expert")),
        P("expert", None, "dp"),
        P("expert", "dp", None),
        P(("dp", "expert"), None),
    )
    out_specs = (
        P(("dp", "expert"), None),
        P(("dp", "expert")),
        P(("dp", "expert"), None),
        P("expert", None, "dp"),
        P("expert", "dp", None),
    )
    return jax.shard_map(local, mesh=mesh, in_specs=in_specs, out_specs=out_specs, check_vma=False)
```

```python
import functools

import jax
import jax.numpy as jnp
from jax import lax
from jax.experimental import pallas as pl
from jax.experimental.pallas import tpu as pltpu
from jax.sharding import PartitionSpec as P

root_half = 0.7071067811865476
inv_root_tau = 0.3989422804014327
MESH = pl.DeviceIdType.MESH
CAP = 8
UNIT = 2 * CAP
NY = 4
CHUNKS = 4
LAST = CHUNKS - 1
BF16, F32 = jnp.bfloat16, jnp.float32


def layer_kernel(
    plane,
    tok, cot, gate, ids, win_h, wout_h,
    mixed, ggrad, tgrad, dwin_h, dwout_h,
    XG, win, wout, S, H, Pf, sib, rs, rs_raw, stage, aback, aback_all, gown, sibx, sibg, all_ids, placers,
    swap_s, swap_r, w_s, a2a_s, a2a_r, ag_s, ag_r, sb_s, sb_r, ps_s, ps_r, rs_s, rs_r,
    bk_s, bk_r, fn_s, fn_r, out_s, ids_s, ids_r, raw_s, raw_r, rt_s, rt_r, ab_s, ab_r, bb_s, bb_r, ft_s, ft_r, credit,
):
    tokens, features = tok.shape
    block = UNIT * plane
    rows_all = NY * block
    hidden_width = win.shape[2]
    tile_rows = rows_all // 2
    quarter = features // CHUNKS
    eighth = quarter // 2
    X, G = XG.at[0], XG.at[1]

    dp = lax.axis_index("dp")
    e = lax.axis_index("expert")
    y = dp // 2
    c = dp % 2
    o = 1 - c
    y_up, y_dn, y_far = (y + 1) % NY, (y + 3) % NY, (y + 2) % NY
    up, dn, twin = y_up * 2 + c, y_dn * 2 + c, y * 2 + o

    def remote(src, dst, ssem, rsem, to_dp, to_e=None):
        return pltpu.make_async_remote_copy(
            src_ref=src, dst_ref=dst, send_sem=ssem, recv_sem=rsem,
            device_id=(to_dp, e if to_e is None else to_e), device_id_type=MESH,
        )

    def wait_in(ref, sem):
        remote(ref, ref, sem, sem, dp).wait_recv()

    def wait_out(ref, sem):
        remote(ref, ref, sem, sem, dp).wait_send()

    def cols(k):
        return pl.ds(k * quarter, quarter)

    def part(k, h):
        return pl.ds(k * quarter + h * eighth, eighth)

    def block_rows(yb):
        return pl.ds(pl.multiple_of(yb * block, block), block)

    def unit_rows(start):
        return pl.ds(pl.multiple_of(start, UNIT), UNIT)

    load_in = pltpu.make_async_copy(win_h, win, w_s.at[0])
    load_out = pltpu.make_async_copy(wout_h, wout, w_s.at[1])

    barrier = pltpu.get_barrier_semaphore()

    def greet(k, carry):
        pl.semaphore_signal(barrier, inc=1, device_id=(dp, (e + k) % plane), device_id_type=MESH)
        return carry

    def greet_dp(k, carry):
        pl.semaphore_signal(barrier, inc=1, device_id=((dp + k) % (2 * NY), e), device_id_type=MESH)
        return carry

    lax.fori_loop(1, 2 * NY, greet_dp, 0)
    lax.fori_loop(1, plane, greet, 0)

    diagonal = lax.broadcasted_iota(jnp.int32, (tokens, tokens), 0) == lax.broadcasted_iota(
        jnp.int32, (tokens, tokens), 1
    )
    gate_col = jnp.sum(jnp.where(diagonal, gate[...], 0.0), 1, keepdims=True)
    gown[...] = (gate_col * cot[...].astype(F32)).astype(BF16)

    def placer_of(id_row, core):
        n_experts = 2 * plane
        onehot = lax.broadcasted_iota(jnp.int32, (n_experts, tokens), 0) == id_row
        onehot_f = onehot.astype(F32)
        before = (
            lax.broadcasted_iota(jnp.int32, (tokens, tokens), 0)
            < lax.broadcasted_iota(jnp.int32, (tokens, tokens), 1)
        ).astype(F32).astype(BF16)
        rank = jnp.dot(onehot_f.astype(BF16), before, preferred_element_type=F32)
        slot = jnp.sum(rank * onehot_f, 0, keepdims=True).astype(jnp.int32)
        target = (id_row >> 1) * UNIT + core * CAP + slot
        target = jnp.where((id_row & 1) == c, target, -1)
        return (lax.broadcasted_iota(jnp.int32, (block, tokens), 0) == target).astype(F32).astype(BF16)

    placers[0, y] = placer_of(ids[...], c)
    pl.semaphore_wait(barrier, plane - 1 + 2 * NY - 1)

    for k in range(1, 2 * NY):
        remote(ids, all_ids.at[dp], ids_s.at[k], ids_r.at[k], (dp + k) % (2 * NY)).start()
    swap = [
        remote(tok, sibx, swap_s.at[0], swap_r.at[0], twin),
        remote(gown, sibg, swap_s.at[1], swap_r.at[1], twin),
    ]

    own_src = (tok, gown)
    sib_src = (sibx, sibg)
    chunks = [(a, k) for a in range(2) for k in range(CHUNKS)]

    blocks_y = (y, y_up, y_dn, y_far)

    def raw_rows(core, yb):
        return pl.ds(pl.multiple_of((core * NY + yb) * tokens, tokens), tokens)

    def raw_at(a, core, yb, h):
        return Pf.at[a, raw_rows(core, yb), pl.ds(h * eighth, eighth)]

    def raw_own(a):
        for h in range(2):
            for n, to in ((h, up), (2 + h, dn)):
                remote(
                    own_src[a].at[:, part(LAST, h)], raw_at(a, c, y, h), raw_s.at[a, n], raw_r.at[a, n], to
                ).start()

    def raw_to_twin(a, i):
        yb, h = raw_pieces[i]
        ref = raw_at(a, c, yb, h)
        remote(ref, ref, rt_s.at[a, i], rt_r.at[a, i], twin).start()

    raw_pieces = ((y_dn, 0), (y_dn, 1), (y_up, 0), (y_up, 1), (y_far, 0), (y_far, 1))

    def raw_forward(a):
        for i, n, to in ((0, 4, up), (3, 5, dn)):
            ref = raw_at(a, c, *raw_pieces[i])
            wait_in(ref, raw_r.at[a, i])
            remote(ref, ref, raw_s.at[a, n], raw_r.at[a, n], to).start()
            raw_to_twin(a, i)

    def raw_rest(a):
        for i in (1, 2, 4, 5):
            wait_in(raw_at(a, c, *raw_pieces[i]), raw_r.at[a, i])
            raw_to_twin(a, i)

    def raw_wait_twin(a):
        for i in range(6):
            wait_in(raw_at(a, o, *raw_pieces[i]), rt_r.at[a, i])

    def raw_wait_sends(a):
        for i in range(6):
            wait_out(raw_at(a, c, y, 0), raw_s.at[a, i])
            wait_out(raw_at(a, c, y, 0), rt_s.at[a, i])

    def wide_stage(a, yb):
        if a == 0:
            return Pf.at[0, block_rows(yb), pl.ds(quarter, quarter)]
        return sib.at[block_rows(yb), pl.ds(0, quarter)]

    def wide_place(a):
        for j, yb in enumerate(blocks_y):
            if j == 0:
                mine, theirs = own_src[a][:, cols(LAST)], sib_src[a][:, cols(LAST)]
            else:
                mine = Pf[a, raw_rows(c, yb), pl.ds(0, quarter)]
                theirs = Pf[a, raw_rows(o, yb), pl.ds(0, quarter)]
            placed = jnp.dot(placers[0, yb], mine, preferred_element_type=F32)
            placed += jnp.dot(placers[1, yb], theirs, preferred_element_type=F32)
            wide_stage(a, yb)[...] = placed.astype(BF16)

    def wide_scatter(a, j):
        yb = blocks_y[j]
        landing = XG.at[a, c, unit_rows(yb * block + e * UNIT), cols(LAST)]
        source = wide_stage(a, yb)
        pltpu.make_async_copy(source.at[unit_rows(e * UNIT)], landing, ab_r.at[a, j]).start()

        def send(step, carry):
            to = (e + step) % plane
            remote(source.at[unit_rows(to * UNIT)], landing, ab_s.at[a, j], ab_r.at[a, j], dp, to).start()
            return carry

        lax.fori_loop(1, plane, send, 0)

    def wide_wait_sends(a):
        for j in range(NY):
            wait_out(wide_stage(a, y).at[pl.ds(0, UNIT * (plane - 1))], ab_s.at[a, j])

    def wide_arrived(a, j):
        ref = XG.at[a, c, block_rows(blocks_y[j]), cols(LAST)]
        wait_in(ref, ab_r.at[a, j])
        remote(ref, ref, sb_s.at[a, LAST, j], sb_r.at[a, LAST, j], twin).start()

    def place(q):
        a, k = chunks[q]
        placed = jnp.dot(placers[0, y], own_src[a][:, cols(k)], preferred_element_type=F32)
        placed += jnp.dot(placers[1, y], sib_src[a][:, cols(k)], preferred_element_type=F32)
        stage[a, :, cols(k)] = placed.astype(BF16)

    def scatter(q):
        a, k = chunks[q]
        landing = XG.at[a, c, unit_rows(y * block + e * UNIT), cols(k)]
        pltpu.make_async_copy(stage.at[a, unit_rows(e * UNIT), cols(k)], landing, a2a_r.at[a, k]).start()

        def send(step, carry):
            to = (e + step) % plane
            remote(
                stage.at[a, unit_rows(to * UNIT), cols(k)], landing, a2a_s.at[a, k], a2a_r.at[a, k], dp, to
            ).start()
            return carry

        lax.fori_loop(1, plane, send, 0)

    ring_pieces = ((y_dn, 0), (y_dn, 1), (y_up, 0), (y_up, 1), (y_far, 0), (y_far, 1))

    def piece(q, f, where):
        a, k = chunks[q]
        return XG.at[a, f, block_rows(where[0]), part(k, where[1])]

    def to_twin(q, n, where):
        a, k = chunks[q]
        ref = piece(q, c, where)
        remote(ref, ref, sb_s.at[a, k, n], sb_r.at[a, k, n], twin).start()

    def send_own(q):
        a, k = chunks[q]
        wait_in(XG.at[a, c, block_rows(y), cols(k)], a2a_r.at[a, k])
        for h in range(2):
            for n, to in ((h, up), (2 + h, dn)):
                ref = piece(q, c, (y, h))
                remote(ref, ref, ag_s.at[a, k, n], ag_r.at[a, k, n], to).start()
        for h in range(2):
            to_twin(q, 6 + h, (y, h))

    def forward_on(q):
        a, k = chunks[q]
        for i, n, to in ((0, 4, up), (3, 5, dn)):
            ref = piece(q, c, ring_pieces[i])
            wait_in(ref, ag_r.at[a, k, i])
            remote(ref, ref, ag_s.at[a, k, n], ag_r.at[a, k, n], to).start()
            to_twin(q, i, ring_pieces[i])

    def take_rest(q):
        a, k = chunks[q]
        for i in (1, 2, 4, 5):
            wait_in(piece(q, c, ring_pieces[i]), ag_r.at[a, k, i])
            to_twin(q, i, ring_pieces[i])

    def wait_twin(a):
        for j in range(NY):
            wait_in(XG.at[a, o, block_rows(blocks_y[j]), cols(LAST)], sb_r.at[a, LAST, j])
        for k in range(LAST):
            q = a * CHUNKS + k
            for n, where in enumerate(ring_pieces + ((y, 0), (y, 1))):
                wait_in(piece(q, o, where), sb_r.at[a, k, n])

    def wait_gather_sends(a):
        for j in range(NY):
            wait_out(XG.at[a, c, block_rows(y), cols(LAST)], sb_s.at[a, LAST, j])
        for k in range(LAST):
            q = a * CHUNKS + k
            for n in range(6):
                wait_out(piece(q, c, (y, 0)), ag_s.at[a, k, n])
            for n in range(8):
                wait_out(piece(q, c, (y, 0)), sb_s.at[a, k, n])

    def tile(t):
        return pl.ds(pl.multiple_of(t * tile_rows, tile_rows), tile_rows)

    def forward(f, t):
        rows = tile(t)
        pre = jnp.dot(X[f, rows, :], win[f], preferred_element_type=F32)
        cdf = 0.5 * (1.0 + lax.erf(pre * root_half))
        hid = (pre * cdf).astype(BF16)
        H[f, rows, :] = hid
        S[f, rows, :] = (cdf + pre * jnp.exp(-0.5 * pre * pre) * inv_root_tau).astype(BF16)
        for k in range(CHUNKS):
            Pf[f, rows, cols(k)] = jnp.dot(hid, wout[f, :, cols(k)], preferred_element_type=F32).astype(BF16)

    sums = (Pf, G)

    def partial_to_twin(d, k):
        remote(sums[d].at[o, :, cols(k)], sib.at[:, cols(k)], ps_s.at[d, k], ps_r.at[d, k], twin).start()

    def wait_partial_sends(d):
        for k in range(CHUNKS):
            wait_out(sib.at[:, cols(k)], ps_s.at[d, k])

    def rs_send(d, k, i, where, to):
        ref = sums[d].at[c, block_rows(where[0]), part(k, where[1])]
        remote(ref, rs.at[d, k, i], rs_s.at[d, k, i], rs_r.at[d, k, i], to).start()

    def add_twin(d, k, yb):
        rows = block_rows(yb)
        sums[d][c, rows, cols(k)] = (
            sums[d][c, rows, cols(k)].astype(F32) + sib[rows, cols(k)].astype(F32)
        ).astype(BF16)

    def add_ring(d, k, where, i):
        wait_in(rs.at[d, k, i], rs_r.at[d, k, i])
        rows, at = block_rows(where[0]), part(k, where[1])
        sums[d][c, rows, at] = (sums[d][c, rows, at].astype(F32) + rs[d, k, i].astype(F32)).astype(BF16)

    def reduce_start(d, k):
        wait_in(sib.at[:, cols(k)], ps_r.at[d, k])
        add_twin(d, k, y_far)
        rs_send(d, k, 0, (y_far, 0), up)
        rs_send(d, k, 3, (y_far, 1), dn)
        add_twin(d, k, y_up)
        rs_send(d, k, 1, (y_up, 1), up)
        add_twin(d, k, y_dn)
        rs_send(d, k, 4, (y_dn, 0), dn)
        add_twin(d, k, y)

    def reduce_middle(d, k):
        add_ring(d, k, (y_up, 0), 0)
        rs_send(d, k, 2, (y_up, 0), up)
        add_ring(d, k, (y_dn, 1), 3)
        rs_send(d, k, 5, (y_dn, 1), dn)

    def reduce_end(d, k):
        rows = block_rows(y)
        for h, ins in enumerate(((4, 2), (1, 5))):
            for i in ins:
                wait_in(rs.at[d, k, i], rs_r.at[d, k, i])
            at = part(k, h)
            sums[d][c, rows, at] = (
                sums[d][c, rows, at].astype(F32) + rs[d, k, ins[0]].astype(F32) + rs[d, k, ins[1]].astype(F32)
            ).astype(BF16)

        def leaving(to):
            return sums[d].at[c, unit_rows(y * block + to * UNIT), cols(k)]

        landing = aback.at[d, unit_rows(e * UNIT), cols(k)]
        pltpu.make_async_copy(leaving(e), landing, bk_r.at[d, k]).start()

        def send(step, carry):
            to = (e + step) % plane
            remote(leaving(to), landing, bk_s.at[d, k], bk_r.at[d, k], dp, to).start()
            return carry

        lax.fori_loop(1, plane, send, 0)

    kept = (mixed, tgrad)
    other_sum = (sibx, sibg)

    def unplace(d, k):
        wait_in(aback.at[d, :, cols(k)], bk_r.at[d, k])
        routed = aback[d, :, cols(k)]
        dims = (((0,), (0,)), ((), ()))
        leave = stage.at[d, pl.ds(0, tokens), cols(k)]
        leave[...] = lax.dot_general(placers[1, y], routed, dims, preferred_element_type=F32).astype(BF16)
        remote(leave, other_sum[d].at[:, cols(k)], fn_s.at[d, k], fn_r.at[d, k], twin).start()
        kept[d][:, cols(k)] = lax.dot_general(placers[0, y], routed, dims, preferred_element_type=F32).astype(BF16)

    def wide_leave(d):
        wait_in(sib.at[:, cols(LAST)], ps_r.at[d, LAST])
        for j, yb in enumerate(blocks_y):
            add_twin(d, LAST, yb)
            landing = aback_all.at[d, yb, unit_rows(e * UNIT)]
            source = sums[d].at[c, block_rows(yb), cols(LAST)]
            pltpu.make_async_copy(source.at[unit_rows(e * UNIT)], landing, bb_r.at[d, j]).start()

            def send(step, carry, j=j, landing=landing, source=source):
                to = (e + step) % plane
                remote(source.at[unit_rows(to * UNIT)], landing, bb_s.at[d, j], bb_r.at[d, j], dp, to).start()
                return carry

            lax.fori_loop(1, plane, send, 0)

    def raw_in(d, yb):
        return S.at[d, pl.ds(pl.multiple_of(yb * tokens, tokens), tokens), pl.ds(0, quarter)]

    def wide_unplace(d):
        dims = (((0,), (0,)), ((), ()))
        for j, yb in enumerate(blocks_y):
            wait_in(aback_all.at[d, yb], bb_r.at[d, j])
            routed = aback_all[d, yb]
            mine = lax.dot_general(placers[0, yb], routed, dims, preferred_element_type=F32).astype(BF16)
            theirs = lax.dot_general(placers[1, yb], routed, dims, preferred_element_type=F32).astype(BF16)
            aback_all[d, yb, pl.ds(0, tokens)] = mine
            leave = aback_all.at[d, yb, pl.ds(tokens, tokens)]
            leave[...] = theirs
            remote(leave, raw_in(d, yb), ft_s.at[d, j], ft_r.at[d, j], twin).start()

    def raw_total(d, where):
        return aback_all.at[d, where[0], pl.ds(0, tokens), pl.ds(where[1] * eighth, eighth)]

    def raw_send(d, i, where, to):
        remote(raw_total(d, where), rs_raw.at[d, i], rs_s.at[d, LAST, i], rs_r.at[d, LAST, i], to).start()

    def raw_add(d, where, i):
        wait_in(rs_raw.at[d, i], rs_r.at[d, LAST, i])
        ref = raw_total(d, where)
        ref[...] = (ref[...].astype(F32) + rs_raw[d, i].astype(F32)).astype(BF16)

    def raw_sum_start(d):
        for j in (3, 1, 2, 0):
            yb = blocks_y[j]
            wait_in(raw_in(d, yb), ft_r.at[d, j])
            own = aback_all.at[d, yb, pl.ds(0, tokens)]
            own[...] = (own[...].astype(F32) + raw_in(d, yb)[...].astype(F32)).astype(BF16)
        raw_send(d, 0, (y_far, 0), up)
        raw_send(d, 3, (y_far, 1), dn)
        raw_send(d, 1, (y_up, 1), up)
        raw_send(d, 4, (y_dn, 0), dn)

    def raw_sum_middle(d):
        raw_add(d, (y_up, 0), 0)
        raw_send(d, 2, (y_up, 0), up)
        raw_add(d, (y_dn, 1), 3)
        raw_send(d, 5, (y_dn, 1), dn)

    def raw_sum_end(d):
        for h, ins in enumerate(((4, 2), (1, 5))):
            for i in ins:
                wait_in(rs_raw.at[d, i], rs_r.at[d, LAST, i])
            kept[d][:, part(LAST, h)] = (
                raw_total(d, (y, h))[...].astype(F32) + rs_raw[d, ins[0]].astype(F32) + rs_raw[d, ins[1]].astype(F32)
            ).astype(BF16)

    def token_rows(d, k):
        if k == LAST:
            return kept[d][:, cols(k)].astype(F32)
        wait_in(other_sum[d].at[:, cols(k)], fn_r.at[d, k])
        return kept[d][:, cols(k)].astype(F32) + other_sum[d][:, cols(k)].astype(F32)

    transposed = (((1,), (1,)), ((), ()))
    over_rows = (((0,), (0,)), ((), ()))

    def hidden_back(f):
        def step(t, carry):
            rows = tile(t)
            back = lax.dot_general(G[f, rows, :], wout[f], transposed, preferred_element_type=F32)
            H[f, rows, :] = (back * S[f, rows, :].astype(F32)).astype(BF16)
            return carry

        lax.fori_loop(0, 2, step, 0)

    def token_back(f, k):
        def step(t, carry):
            rows = tile(t)
            G[f, rows, cols(k)] = lax.dot_general(
                H[f, rows, :], win[f, cols(k), :], transposed, preferred_element_type=F32
            ).astype(BF16)
            return carry

        lax.fori_loop(0, 2, step, 0)

    def out_tiles(f):
        def step(n, carry):
            at = pl.ds(pl.multiple_of(n * quarter, quarter), quarter)
            Pf[o, pl.ds(pl.multiple_of(f * hidden_width, hidden_width), hidden_width), at] = lax.dot_general(
                H[f], G[f, :, at], over_rows, preferred_element_type=F32
            ).astype(BF16)
            return carry

        lax.fori_loop(0, CHUNKS, step, 0)

    def in_weights_spot(f, m):
        return (
            o,
            pl.ds(pl.multiple_of(f * quarter, quarter), quarter),
            pl.ds(pl.multiple_of(m * hidden_width, hidden_width), hidden_width),
        )

    def in_copy(f, m):
        return pltpu.make_async_copy(
            Pf.at[in_weights_spot(f, m)], dwin_h.at[f, pl.ds(m * quarter, quarter)], out_s.at[2 + CHUNKS * f + m]
        )

    def in_tiles(f):
        def step(m, carry):
            at = pl.ds(pl.multiple_of(m * quarter, quarter), quarter)
            Pf[in_weights_spot(f, m)] = lax.dot_general(
                X[f, :, at], H[f], over_rows, preferred_element_type=F32
            ).astype(BF16)
            return carry

        lax.fori_loop(0, CHUNKS, step, 0)
        for m in range(CHUNKS):
            in_copy(f, m).start()

    swap[0].start()
    raw_own(0)
    swap[1].start()
    raw_own(1)
    load_in.start()
    load_out.start()

    for k in range(1, 2 * NY):
        wait_in(all_ids.at[(dp + 2 * NY - k) % (2 * NY)], ids_r.at[k])
    placers[1, y] = placer_of(all_ids[twin], o)
    swap[0].wait_recv()
    place(0)
    scatter(0)
    for yb in (y_dn, y_up, y_far):
        placers[0, yb] = placer_of(all_ids[yb * 2 + c], c)
        placers[1, yb] = placer_of(all_ids[yb * 2 + o], o)
    raw_forward(0)
    place(1)
    send_own(0)
    scatter(1)
    raw_rest(0)
    raw_forward(1)
    place(2)
    send_own(1)
    scatter(2)
    forward_on(0)
    raw_wait_twin(0)
    wide_place(0)
    wide_scatter(0, 0)
    wide_scatter(0, 1)
    swap[1].wait_recv()
    place(4)
    place(5)
    place(6)
    take_rest(0)
    send_own(2)
    scatter(4)
    wide_scatter(0, 2)
    wide_scatter(0, 3)
    forward_on(1)
    raw_rest(1)
    raw_wait_twin(1)
    wide_place(1)
    scatter(5)
    take_rest(1)
    forward_on(2)
    wide_arrived(0, 0)
    wide_arrived(0, 1)
    send_own(4)
    scatter(6)
    wide_scatter(1, 0)
    take_rest(2)
    wide_arrived(0, 2)
    wide_arrived(0, 3)
    wide_scatter(1, 1)
    send_own(5)
    wide_scatter(1, 2)
    wide_scatter(1, 3)
    raw_wait_sends(0)
    raw_wait_sends(1)
    wide_wait_sends(0)
    load_in.wait()
    load_out.wait()
    wait_twin(0)
    forward(o, 0)
    forward_on(4)
    send_own(6)
    take_rest(4)
    forward_on(5)
    wide_arrived(1, 0)
    wide_arrived(1, 1)
    forward(o, 1)
    wide_arrived(1, 2)
    wide_arrived(1, 3)
    wide_wait_sends(1)
    pl.semaphore_signal(credit, inc=1, device_id=(twin, e), device_id_type=MESH)
    pl.semaphore_wait(credit, 1)
    for k in (LAST, 0, 1, 2):
        partial_to_twin(0, k)
    take_rest(5)
    forward_on(6)
    forward(c, 0)
    take_rest(6)
    forward(c, 1)

    reduce_start(0, 0)
    wide_leave(0)
    reduce_start(0, 1)
    wait_partial_sends(0)
    wait_twin(1)
    out_tiles(o)
    reduce_middle(0, 0)
    out_tiles(c)
    out_copies = [
        pltpu.make_async_copy(Pf.at[o, pl.ds(f * hidden_width, hidden_width)], dwout_h.at[f], out_s.at[f])
        for f in range(2)
    ]
    for copy in out_copies:
        copy.start()
    reduce_start(0, 2)
    pl.semaphore_signal(credit, inc=1, device_id=(twin, e), device_id_type=MESH)
    reduce_middle(0, 1)
    hidden_back(o)
    reduce_end(0, 0)
    hidden_back(c)
    wait_gather_sends(1)
    pl.semaphore_wait(credit, 1)
    token_back(o, LAST)
    partial_to_twin(1, LAST)
    token_back(c, LAST)
    reduce_middle(0, 2)
    token_back(o, 0)
    partial_to_twin(1, 0)
    token_back(c, 0)
    wide_leave(1)
    wide_unplace(0)
    reduce_start(1, 0)
    token_back(o, 1)
    partial_to_twin(1, 1)
    token_back(c, 1)
    reduce_end(0, 1)
    raw_sum_start(0)
    token_back(o, 2)
    partial_to_twin(1, 2)
    token_back(c, 2)
    reduce_start(1, 1)
    reduce_end(0, 2)
    reduce_middle(1, 0)
    raw_sum_middle(0)

    sent_rows = UNIT * (plane - 1)
    for a in range(2):
        for k in range(LAST):
            wait_out(stage.at[a, pl.ds(0, sent_rows), cols(k)], a2a_s.at[a, k])
    for copy in swap:
        copy.wait_send()
    for copy in out_copies:
        copy.wait()
    unplace(0, 0)
    reduce_start(1, 2)
    reduce_middle(1, 1)
    in_tiles(0)
    wide_unplace(1)
    raw_sum_start(1)
    reduce_end(1, 0)
    unplace(0, 1)
    reduce_middle(1, 2)
    raw_sum_end(0)
    in_tiles(1)
    reduce_end(1, 1)
    unplace(0, 2)
    raw_sum_middle(1)
    gate_total = jnp.zeros((tokens, 1), F32)
    for k in range(CHUNKS):
        out_rows = token_rows(0, k)
        gate_total += jnp.sum(cot[:, cols(k)].astype(F32) * out_rows, 1, keepdims=True)
        mixed[:, cols(k)] = (gate_col * out_rows).astype(BF16)
    ggrad[...] = jnp.sum(jnp.where(diagonal, gate_total, 0.0), 0, keepdims=True)
    unplace(1, 0)
    reduce_end(1, 2)
    raw_sum_end(1)
    unplace(1, 1)
    tgrad[:, cols(0)] = token_rows(1, 0).astype(BF16)
    tgrad[:, cols(1)] = token_rows(1, 1).astype(BF16)
    unplace(1, 2)
    tgrad[:, cols(2)] = token_rows(1, 2).astype(BF16)

    wait_gather_sends(0)
    wait_partial_sends(1)
    for f in range(2):
        for m in range(CHUNKS):
            in_copy(f, m).wait()
    for k in range(1, 2 * NY):
        wait_out(ids, ids_s.at[k])
    for d in range(2):
        for i in range(6):
            wait_out(rs_raw.at[d, i], rs_s.at[d, LAST, i])
        for j in range(NY):
            wait_out(aback_all.at[d, y, pl.ds(0, sent_rows)], bb_s.at[d, j])
            wait_out(raw_in(d, y), ft_s.at[d, j])
        for k in range(LAST):
            for i in range(6):
                wait_out(rs.at[d, k, i], rs_s.at[d, k, i])
            wait_out(aback.at[d, pl.ds(0, sent_rows), cols(k)], bk_s.at[d, k])
            wait_out(stage.at[d, pl.ds(0, tokens), cols(k)], fn_s.at[d, k])


def hand_over_kernel(*refs):
    sources, targets, held, sems_in, sems_out = refs[:5], refs[5:10], refs[10:15], refs[15], refs[16]
    pieces = []
    for source, target, mid in zip(sources, targets, held):
        if len(source.shape) == 3:
            half = source.shape[1] // 2
            for f in range(source.shape[0]):
                for n in range(2):
                    at = (f, pl.ds(n * half, half))
                    pieces.append((source.at[at], mid.at[at], target.at[at]))
        else:
            pieces.append((source, mid, target))
    ins = [pltpu.make_async_copy(s, m, sems_in.at[n]) for n, (s, m, t) in enumerate(pieces)]
    outs = [pltpu.make_async_copy(m, t, sems_out.at[n]) for n, (s, m, t) in enumerate(pieces)]
    for copy in ins:
        copy.start()
    for arrived, leaving in zip(ins, outs):
        arrived.wait()
        leaving.start()
    for copy in outs:
        copy.wait()


def local(tokens, expert_ids, gate_weights, in_weights, out_weights, cotangent):
    plane = lax.axis_size("expert")
    count, features = tokens.shape
    hidden_width = in_weights.shape[2]
    block = UNIT * plane
    rows_all = NY * block
    quarter = features // CHUNKS
    vmem = pl.BlockSpec(memory_space=pltpu.VMEM)
    hbm = pl.BlockSpec(memory_space=pl.ANY)
    dma = pltpu.SemaphoreType.DMA
    shapes = (
        jax.ShapeDtypeStruct((count, features), BF16),
        jax.ShapeDtypeStruct((1, count), F32),
        jax.ShapeDtypeStruct((count, features), BF16),
        jax.ShapeDtypeStruct(in_weights.shape, BF16),
        jax.ShapeDtypeStruct(out_weights.shape, BF16),
    )
    results = pl.pallas_call(
        functools.partial(layer_kernel, plane),
        out_shape=shapes,
        in_specs=[vmem, vmem, vmem, vmem, hbm, hbm],
        out_specs=(vmem, vmem, vmem, hbm, hbm),
        scratch_shapes=[
            pltpu.VMEM((2, 2, rows_all, features), BF16),
            pltpu.VMEM(in_weights.shape, BF16),
            pltpu.VMEM(out_weights.shape, BF16),
            pltpu.VMEM((2, rows_all, hidden_width), BF16),
            pltpu.VMEM((2, rows_all, hidden_width), BF16),
            pltpu.VMEM((2, rows_all, features), BF16),
            pltpu.VMEM((rows_all, features), BF16),
            pltpu.VMEM((2, LAST, 6, block, quarter // 2), BF16),
            pltpu.VMEM((2, 6, count, quarter // 2), BF16),
            pltpu.VMEM((2, block, LAST * quarter), BF16),
            pltpu.VMEM((2, block, LAST * quarter), BF16),
            pltpu.VMEM((2, NY, block, quarter), BF16),
            pltpu.VMEM((count, features), BF16),
            pltpu.VMEM((count, features), BF16),
            pltpu.VMEM((count, features), BF16),
            pltpu.VMEM((2 * NY, 1, count), jnp.int32),
            pltpu.VMEM((2, NY, block, count), BF16),
            dma((2,)), dma((2,)), dma((2,)),
            dma((2, CHUNKS)), dma((2, CHUNKS)),
            dma((2, CHUNKS, 6)), dma((2, CHUNKS, 6)),
            dma((2, CHUNKS, 8)), dma((2, CHUNKS, 8)),
            dma((2, CHUNKS)), dma((2, CHUNKS)),
            dma((2, CHUNKS, 6)), dma((2, CHUNKS, 6)),
            dma((2, CHUNKS)), dma((2, CHUNKS)),
            dma((2, CHUNKS)), dma((2, CHUNKS)),
            dma((2 + 2 * CHUNKS,)),
            dma((2 * NY,)), dma((2 * NY,)),
            dma((2, 6)), dma((2, 6)),
            dma((2, 6)), dma((2, 6)),
            dma((2, NY)), dma((2, NY)),
            dma((2, NY)), dma((2, NY)),
            dma((2, NY)), dma((2, NY)),
            pltpu.SemaphoreType.REGULAR,
        ],
        compiler_params=pltpu.CompilerParams(
            collective_id=0, has_side_effects=True, vmem_limit_bytes=60 * 1024 * 1024
        ),
    )(
        tokens, cotangent, gate_weights.reshape(1, count), expert_ids.reshape(1, count), in_weights, out_weights,
    )
    mixed, gate_grad, token_grad, in_grad, out_grad = pl.pallas_call(
        hand_over_kernel,
        out_shape=shapes,
        in_specs=[pl.BlockSpec(memory_space=pltpu.HBM)] * 5,
        out_specs=(pl.BlockSpec(memory_space=pltpu.HBM),) * 5,
        scratch_shapes=[pltpu.VMEM(shape.shape, shape.dtype) for shape in shapes] + [dma((11,)), dma((11,))],
        compiler_params=pltpu.CompilerParams(vmem_limit_bytes=60 * 1024 * 1024),
    )(*results)
    return mixed, gate_grad.reshape(count), token_grad, in_grad, out_grad


def solution(mesh):
    in_specs = (
        P(("dp", "expert"), None),
        P(("dp", "expert")),
        P(("dp", "expert")),
        P("expert", None, "dp"),
        P("expert", "dp", None),
        P(("dp", "expert"), None),
    )
    out_specs = (
        P(("dp", "expert"), None),
        P(("dp", "expert")),
        P(("dp", "expert"), None),
        P("expert", None, "dp"),
        P("expert", "dp", None),
    )
    return jax.shard_map(local, mesh=mesh, in_specs=in_specs, out_specs=out_specs, check_vma=False)
```
